128 devices in a mesh: dp: 4 (over y), ep: 32 (over x, z, core).
Axes of the slice: x: 4, y: 4, z: 4, core: 2. Of those that a mesh axis runs over, the one named last changes fastest.
Arguments:
- tokens: bfloat16 [8192, 2048], P(('dp', 'ep')), may hold values from -6 to 6
- row_counts: int32 [128], P(('dp', 'ep')), may hold values from 1 to 64, 5120 in all
- expert_ids: int32 [8192, 6], P(('dp', 'ep')), may hold values from 0 to 63, all different within a row; in each aligned block of 64 rows (0 to 63, 64 to 127, ...) at most 8 rows name the same one
- gate_weights: float32 [8192, 6], P(('dp', 'ep')), may hold values from 0.1 to 1
- expert_gate: bfloat16 [64, 2048, 1408], P('ep', None, 'dp'), may hold values from -0.125 to 0.125
- expert_up: bfloat16 [64, 2048, 1408], P('ep', None, 'dp'), may hold values from -0.125 to 0.125
- expert_down: bfloat16 [64, 1408, 2048], P('ep', 'dp'), may hold values from -0.15625 to 0.15625
- shared_gate: bfloat16 [2048, 2816], P(None, 'dp'), may hold values from -0.125 to 0.125
- shared_up: bfloat16 [2048, 2816], P(None, 'dp'), may hold values from -0.125 to 0.125
- shared_down: bfloat16 [2816, 2048], P('dp'), may hold values from -0.109375 to 0.109375
Outputs:
- mixed: bfloat16 [8192, 2048], P(('dp', 'ep'))
The draws below stay inside these ranges and needn't reach their ends.
Inputs may be any that keep to these rules, and one draw needn't show every extreme that they name: `expert_ids`: in each device's block of 64 rows no expert is named by more than 8 rows, a bound that some block reaches; a row names 6 different experts. `row_counts`: some device's slots are all live.
All inputs are finite; a program needn't handle non-finite values.
Results may differ from the reference program's by a relative error of at most 0.012.
Values may be sent and summed in bfloat16 or wider, within the bound.
No kernel may reach another device: no remote copies, remote signals or barrier semaphores. Data moves between devices by JAX's collectives and lax.ppermute only.
A program may use at most 128 MiB of HBM per device.

```python
import math
import jax
import jax.numpy as jnp
import numpy as np
from jax import lax

D = 2048
FFE = 1408
SHARED = 2816
TOP = 6
TOK_DEV = 64
EXPERTS = 64
TOKENS = 8192
CAP = 8
N_DP = 4
N_EP = 32
DEVICES = 128


def block_levels(rng, dims, pieces, least, high):
    level = 1.0
    for position, shards_of in pieces:
        heights = jax.random.uniform(jax.random.fold_in(jax.random.fold_in(rng, 6), position), (shards_of,), jnp.float32, least / len(pieces), high / len(pieces))
        level = level * jnp.repeat(jnp.exp(heights), dims[position] // shards_of).reshape((-1,) + (1,) * (len(dims) - 1 - position))
    return level


def profile(number_of, total, reach, skew):
    weights = [(1 << 20) // math.isqrt(rank ** skew) + 1 for rank in range(2, number_of + 1)]
    spare, holding = total - reach - (number_of - 1), [1] * (number_of - 1)
    while spare > 0:
        movable = [i for i in range(number_of - 1) if holding[i] < reach]
        whole, left = sum([weights[i] for i in movable]), spare
        for i in movable:
            more = min(reach - holding[i], max(1, left * weights[i] // whole), spare)
            holding[i] = holding[i] + more
            spare = spare - more
    return np.array([reach] + holding)


def uneven_parts(rng, count, total, limit, skew):
    if count == 2:
        one = jax.random.randint(rng, (), max(1, total - limit), min(limit, total - 1) + 1)
        return jnp.stack([one, total - one])
    tallies = jnp.asarray(profile(count, total, limit, skew), jnp.int32)
    twos = (count - 1) // 2
    donor, taker = tallies[1:1 + 2 * twos:2], tallies[2:2 + 2 * twos:2]
    room = jnp.minimum(donor - 1, limit - taker)
    shifted = jax.random.randint(jax.random.fold_in(rng, 1), (twos,), 0, 1 << 20) % (room + 1)
    tallies = tallies.at[1:1 + 2 * twos:2].set(donor - shifted).at[2:2 + 2 * twos:2].set(taker + shifted)
    return tallies[jax.random.permutation(jax.random.fold_in(rng, 2), count)]


def shared_out(stream_key, own, number, rows, number_of, top, limit, skew):
    order = jax.random.permutation(stream_key, number_of)
    heavy_load, usual = portions_of(number_of, rows * top, limit, skew, True), portions_of(number_of, rows * top, limit, skew, False)
    places = jnp.arange(number_of)

    def named(lengths, offset_by):
        used = int((lengths > 0).sum())
        fixed = max(1, used // 4)
        moved = fixed + (places - fixed + offset_by * (used - fixed)) % max(1, number_of - fixed)
        return jnp.zeros((number_of,), jnp.int32).at[order[jnp.where(places < fixed, places, moved)]].set(jnp.asarray(lengths, jnp.int32))

    lengths = jnp.where(number % 4 == 0, named(heavy_load, number // 4), named(usual, number - number // 4 - 1))
    mixed = jax.random.permutation(jax.random.fold_in(own, 3), number_of)
    donor, taker = mixed[0:number_of // 2 * 2:2], mixed[1:number_of // 2 * 2:2]
    margin = jnp.minimum(lengths[donor] - 1, limit - lengths[taker]) // 2
    margin = jnp.where((donor == order[0]) | (taker == order[0]) | (lengths[taker] == 0), 0, jnp.maximum(margin, 0))
    moved = jax.random.randint(jax.random.fold_in(own, 4), (number_of // 2,), 0, 1 << 20) % (margin + 1)
    lengths = lengths.at[donor].add(-moved).at[taker].add(moved)
    labels = jnp.searchsorted(jnp.cumsum(lengths), jnp.arange(rows * top), side="right").astype(jnp.int32)
    listing = labels.reshape(top, rows).T
    listing = listing[jax.random.permutation(jax.random.fold_in(own, 1), rows)]
    offset_by = jax.random.randint(jax.random.fold_in(own, 2), (rows, 1), 0, top)
    return jnp.take_along_axis(listing, (jnp.arange(top)[None, :] + offset_by) % top, axis=1)


def portions_of(number_of, total, reach, lean, full):
    weights = [(1 << 20) // math.isqrt(rank ** lean) + 1 for rank in range(1, number_of + 1)]
    largest = reach if full else min(reach, max(-(-total // number_of), total * weights[0] // sum(weights)))
    least = 1 if total - largest >= number_of - 1 else 0
    counts, rest = [largest] + [least] * (number_of - 1), total - largest - least * (number_of - 1)
    while rest > 0:
        candidates = [i for i in range(1, number_of) if counts[i] < largest] or [i for i in range(1, number_of) if counts[i] < reach]
        pool, remaining = sum([weights[i] for i in candidates]), rest
        for i in candidates:
            more = min(reach - counts[i], max(1, remaining * weights[i] // pool), rest)
            counts[i] = counts[i] + more
            rest = rest - more
    return np.array(counts)


def bell_draw(own_key, extent, width, bound, split=(), kind=jnp.bfloat16):
    loudness = block_levels(own_key, extent, split, -0.22, 0.18) if split else 1.0
    array = jax.random.normal(own_key, extent, jnp.float32) * width * loudness
    return jnp.minimum(jnp.maximum(array, -bound), bound).astype(kind)


def setup_inputs(seed: int = 0) -> dict:
    seeds = jax.random.split(jax.random.key(seed), 11)
    tokens = bell_draw(seeds[0], (TOKENS, D), 1.0, 6.0, ((0, 128),))
    row_counts = uneven_parts(seeds[1], DEVICES, DEVICES * TOK_DEV * 5 // 8, TOK_DEV, 1).astype(jnp.int32)
    expert_ids_keys = jax.random.split(jax.random.fold_in(seeds[2], 1), TOKENS // TOK_DEV)
    expert_ids_turns = jax.random.permutation(jax.random.fold_in(seeds[2], 3), TOKENS // TOK_DEV)
    expert_ids = jax.vmap(lambda own, number: shared_out(jax.random.fold_in(seeds[2], 2), own, number, TOK_DEV, EXPERTS, TOP, CAP, 1))(expert_ids_keys, expert_ids_turns).reshape((TOKENS, TOP))
    gate_weights = jnp.clip(0.1 + 0.9 * jax.random.uniform(seeds[3], (TOKENS, TOP), jnp.float32) ** block_levels(seeds[3], (TOKENS, TOP), ((0, 128),), -0.2, 0.2), 0.1, 1.0)
    expert_gate = bell_draw(seeds[4], (EXPERTS, D, FFE), D ** -0.5, 0.125, ((0, 32), (2, 4)))
    expert_up = bell_draw(seeds[5], (EXPERTS, D, FFE), D ** -0.5, 0.125, ((0, 32), (2, 4)))
    expert_down = bell_draw(seeds[6], (EXPERTS, FFE, D), FFE ** -0.5, 0.15625, ((0, 32), (1, 4)))
    shared_gate = bell_draw(seeds[7], (D, SHARED), D ** -0.5, 0.125, ((1, 4),))
    shared_up = bell_draw(seeds[8], (D, SHARED), D ** -0.5, 0.125, ((1, 4),))
    shared_down = bell_draw(seeds[9], (SHARED, D), SHARED ** -0.5, 0.109375, ((0, 4),))
    return {"tokens": tokens, "row_counts": row_counts, "expert_ids": expert_ids, "gate_weights": gate_weights, "expert_gate": expert_gate, "expert_up": expert_up, "expert_down": expert_down, "shared_gate": shared_gate, "shared_up": shared_up, "shared_down": shared_down}


def slot_tables(expert_ids, gate_weights, row_counts):
    devices = N_DP * N_EP
    per_block = TOK_DEV * TOP
    flat_ids = expert_ids.reshape(devices, per_block)
    flat_gates = gate_weights.reshape(devices, per_block)
    positions = jnp.arange(per_block, dtype=jnp.int32)
    live_slots = (positions // TOP)[None, :] < row_counts[:, None]
    onehot = ((flat_ids[:, :, None] == jnp.arange(EXPERTS, dtype=jnp.int32)[None, None, :]) & live_slots[:, :, None]).astype(jnp.int32)
    before = jnp.cumsum(onehot, axis=1) - onehot
    slot_rank = jnp.sum(before * onehot, axis=2)
    slot_index = jnp.where(live_slots, flat_ids * CAP + slot_rank, EXPERTS * CAP).astype(jnp.int32)
    owners = (jnp.arange(devices, dtype=jnp.int32)[:, None] * TOK_DEV + positions[None, :] // TOP).astype(jnp.int32)

    def fill_block(targets, sources, gates):
        source_row = jnp.full((EXPERTS * CAP,), TOKENS, jnp.int32).at[targets].set(sources, mode="drop")
        slot_gate = jnp.zeros((EXPERTS * CAP,), gates.dtype).at[targets].set(gates, mode="drop")
        return source_row, slot_gate

    source_row, slot_gate = jax.vmap(fill_block)(slot_index, owners, flat_gates)
    source_row = source_row.reshape(devices, EXPERTS, CAP).transpose(1, 0, 2).reshape(EXPERTS, devices * CAP)
    slot_gate = slot_gate.reshape(devices, EXPERTS, CAP).transpose(1, 0, 2).reshape(EXPERTS, devices * CAP)
    return source_row, slot_gate


def expert_apply(rows_in, gate_w, up_w, down_w):
    gate_act = jnp.dot(rows_in, gate_w, preferred_element_type=jnp.float32)
    up_act = jnp.dot(rows_in, up_w, preferred_element_type=jnp.float32)
    hidden = (jax.nn.silu(gate_act) * up_act).astype(jnp.bfloat16)
    quarter = hidden.shape[1] // N_DP
    summed = jnp.zeros((rows_in.shape[0], down_w.shape[1]), jnp.float32)
    for piece_index in range(N_DP):
        partial_value = jnp.dot(hidden[:, piece_index * quarter:(piece_index + 1) * quarter],
                          down_w[piece_index * quarter:(piece_index + 1) * quarter],
                          preferred_element_type=jnp.float32).astype(jnp.bfloat16)
        summed = summed + lax.optimization_barrier(partial_value).astype(jnp.float32)
    return summed


def reference(tokens, row_counts, expert_ids, gate_weights, expert_gate, expert_up, expert_down, shared_gate, shared_up, shared_down):
    padded = jnp.concatenate([tokens, jnp.zeros((1, D), tokens.dtype)], axis=0)
    source_row, slot_gate = slot_tables(expert_ids, gate_weights, row_counts)

    def one_expert(routed, inputs):
        gate_w, up_w, down_w, rows_at, gates_at = inputs
        result = expert_apply(padded[rows_at], gate_w, up_w, down_w)
        return routed.at[rows_at].add(gates_at[:, None] * result, mode="drop"), 0

    routed, unused = lax.scan(one_expert, jnp.zeros((TOKENS, D), jnp.float32),
                              (expert_gate, expert_up, expert_down, source_row, slot_gate))
    shared = expert_apply(tokens, shared_gate, shared_up, shared_down)
    live_rows = (jnp.arange(TOKENS, dtype=jnp.int32) % TOK_DEV) < jnp.repeat(row_counts, TOK_DEV)
    return jnp.where(live_rows[:, None], shared + routed, 0.0).astype(jnp.bfloat16)
```

```python
import functools

import jax
import jax.numpy as jnp
from jax import lax
from jax.experimental import pallas as pl
from jax.experimental.pallas import tpu as pltpu
from jax.sharding import PartitionSpec as P

CAP = 8
SEND_COLS = 1280
BACK_COLS = 1280


def shifted(x, shift, n_dp):
    return lax.ppermute(x, "dp", [(i, (i + shift) % n_dp) for i in range(n_dp)])


def dot_f32(a, b):
    return jnp.dot(a, b, preferred_element_type=jnp.float32)


def split_hi_lo(x):
    hi = x.astype(jnp.bfloat16)
    lo = (x - hi.astype(jnp.float32)).astype(jnp.bfloat16)
    return hi, lo


def expert_kernel(x0, x1, x2, x3, xb, wg, wu, wd, o0, o1, o2, o3, ob):
    dims = (((1,), (1,)), ((), ()))
    for j, (x, o) in enumerate(((x0, o0), (x1, o1), (x2, o2), (x3, o3))):
        cols = x.shape[-1]
        rows_d = x[0]
        rows_b = xb[0, j]

        def project(w):
            return lax.dot_general(
                rows_d, w[0, :, :cols], dims, preferred_element_type=jnp.float32
            ) + lax.dot_general(rows_b, w[0, :, cols:], dims, preferred_element_type=jnp.float32)

        gate = project(wg)
        up = project(wu)
        hidden = (gate / (1.0 + jnp.exp(-gate)) * up).astype(jnp.bfloat16)
        out = jnp.dot(hidden, wd[0], preferred_element_type=jnp.float32).astype(jnp.bfloat16)
        back = o.shape[-1]
        o[0] = out[:, :back]
        ob[0, j] = out[:, back:]


def run_experts(planes, xb, wg, wu, wd, back):
    members, rows, cols = planes[0].shape
    ffe, feature = wg.shape[1:]
    n = len(planes)
    one = lambda shape: pl.BlockSpec((1,) + shape, lambda m: (m,) + (0,) * len(shape))
    return pl.pallas_call(
        expert_kernel,
        grid=(members,),
        in_specs=[one((rows, cols))] * n
        + [one((n, rows, feature - cols))]
        + [one((ffe, feature))] * 3,
        out_specs=[one((rows, back))] * n + [one((n, rows, feature - back))],
        out_shape=[jax.ShapeDtypeStruct((members, rows, back), jnp.bfloat16)] * n
        + [jax.ShapeDtypeStruct((members, n, rows, feature - back), jnp.bfloat16)],
        compiler_params=pltpu.CompilerParams(vmem_limit_bytes=48 * 1024 * 1024),
        cost_estimate=pl.CostEstimate(
            flops=members * n * rows * ffe * feature * 6,
            bytes_accessed=members * (n * rows * feature * 4 + 3 * ffe * feature * 2),
            transcendentals=members * n * rows * ffe,
        ),
    )(*planes, xb, wg, wu, wd)


def on_device(
    tokens,
    row_counts,
    expert_ids,
    gate_weights,
    expert_gate,
    expert_up,
    expert_down,
    shared_gate,
    shared_up,
    shared_down,
):
    tok, feature = tokens.shape
    members = expert_gate.shape[0]
    n_ep = lax.axis_size("ep")
    n_dp = lax.axis_size("dp")
    n_experts = members * n_ep
    sc, bc = SEND_COLS, BACK_COLS

    live = jnp.arange(tok, dtype=jnp.int32) < row_counts[0]
    named = expert_ids[:, :, None] == jnp.arange(n_experts, dtype=jnp.int32)[None, None, :]
    gates = jnp.sum(
        jnp.where(named & live[:, None, None], gate_weights[:, :, None], 0.0), axis=1
    )
    hi, lo = split_hi_lo(gates)
    extended = jnp.concatenate([tokens, hi, lo], axis=1)

    around = [extended] + [shifted(extended, s, n_dp) for s in (1, -1, 2)]
    gathered = jnp.concatenate(around, axis=0)

    def slots_of(hi_cols, blocks):
        rows = blocks * tok
        used = hi_cols > 0
        at = jnp.arange(rows, dtype=jnp.int32)
        earlier = (at[:, None] > at[None, :]) & (at[:, None] // tok == at[None, :] // tok)
        rank = dot_f32(earlier.astype(jnp.bfloat16), used.astype(jnp.bfloat16))
        code = jnp.where(used, rank, -1.0).T.astype(jnp.int32)
        want = jnp.arange(CAP, dtype=jnp.int32)
        block = at // tok
        hit = (code[:, None, None, :] == want[None, None, :, None]) & (
            block[None, None, None, :] == jnp.arange(blocks, dtype=jnp.int32)[None, :, None, None]
        )
        return hit.reshape(n_experts * blocks * CAP, rows)

    hit_d = slots_of(hi, 1)
    send_d = dot_f32(hit_d.astype(jnp.bfloat16), tokens[:, :sc]).astype(jnp.bfloat16)
    came_d = lax.all_to_all(
        send_d.reshape(n_ep, members * CAP, sc), "ep", split_axis=0, concat_axis=0, tiled=True
    )
    own = (
        came_d.reshape(n_ep, members, CAP, sc)
        .transpose(1, 0, 2, 3)
        .reshape(members, n_ep * CAP, sc)
    )
    planes = [own] + [shifted(own, s, n_dp) for s in (1, -1, 2)]

    hit_b = slots_of(gathered[:, feature : feature + n_experts], n_dp)
    send_b = dot_f32(hit_b.astype(jnp.bfloat16), gathered[:, sc:feature]).astype(jnp.bfloat16)
    came_b = lax.all_to_all(
        send_b.reshape(n_ep, members * n_dp * CAP, feature - sc),
        "ep",
        split_axis=0,
        concat_axis=0,
        tiled=True,
    )
    xb = (
        came_b.reshape(n_ep, members, n_dp, CAP, feature - sc)
        .transpose(1, 2, 0, 3, 4)
        .reshape(members, n_dp, n_ep * CAP, feature - sc)
    )

    rows_in = gathered[:, :feature]
    gate_act = dot_f32(rows_in, shared_gate)
    up_act = dot_f32(rows_in, shared_up)
    hidden = (jax.nn.silu(gate_act) * up_act).astype(jnp.bfloat16)
    shared = dot_f32(hidden, shared_down)

    *out_d, out_b = run_experts(
        planes,
        xb,
        expert_gate.swapaxes(1, 2),
        expert_up.swapaxes(1, 2),
        expert_down,
        bc,
    )
    total_d = out_d[0].astype(jnp.float32)
    for j, s in ((1, -1), (2, 1), (3, 2)):
        total_d = total_d + shifted(out_d[j], s, n_dp).astype(jnp.float32)

    back_b = (
        out_b.reshape(members, n_dp, n_ep, CAP, feature - bc)
        .transpose(2, 0, 1, 3, 4)
        .reshape(n_ep, members * n_dp * CAP, feature - bc)
    )
    ret_b = lax.all_to_all(back_b, "ep", split_axis=0, concat_axis=0, tiled=True).reshape(
        n_experts * n_dp * CAP, feature - bc
    )

    def weigh(hit, hi_cols, lo_cols, blocks, values):
        rows = hit.shape[1]
        spread = lambda g: jnp.broadcast_to(
            g.T[:, None, :], (n_experts, blocks * CAP, rows)
        ).reshape(hit.shape)
        contract = (((0,), (0,)), ((), ()))
        zero = jnp.zeros((), jnp.bfloat16)
        parts = [
            lax.dot_general(
                jnp.where(hit, spread(g), zero), values, contract, preferred_element_type=jnp.float32
            )
            for g in (hi_cols, lo_cols)
        ]
        return parts[0] + parts[1]

    routed_b = weigh(
        hit_b,
        gathered[:, feature : feature + n_experts],
        gathered[:, feature + n_experts :],
        n_dp,
        ret_b,
    )
    partial_sum = jnp.concatenate(
        [shared[:, :bc], shared[:, bc:] + routed_b], axis=1
    ).astype(jnp.bfloat16)
    total = partial_sum[:tok].astype(jnp.float32)
    for j, s in ((1, -1), (2, 1), (3, 2)):
        total = total + shifted(partial_sum[j * tok : (j + 1) * tok], s, n_dp).astype(jnp.float32)

    back_d = (
        total_d.astype(jnp.bfloat16)
        .reshape(members, n_ep, CAP, bc)
        .transpose(1, 0, 2, 3)
        .reshape(n_ep, members * CAP, bc)
    )
    ret_d = lax.all_to_all(back_d, "ep", split_axis=0, concat_axis=0, tiled=True).reshape(
        n_experts * CAP, bc
    )
    routed_d = weigh(hit_d, hi, lo, 1, ret_d)
    result = total + jnp.concatenate(
        [routed_d, jnp.zeros((tok, feature - bc), jnp.float32)], axis=1
    )
    return jnp.where(live[:, None], result, 0.0).astype(jnp.bfloat16)


def solution(mesh):
    in_specs = (
        P(("dp", "ep"), None),
        P(("dp", "ep")),
        P(("dp", "ep"), None),
        P(("dp", "ep"), None),
        P("ep", None, "dp"),
        P("ep", None, "dp"),
        P("ep", "dp", None),
        P(None, "dp"),
        P(None, "dp"),
        P("dp", None),
    )
    out_specs = P(("dp", "ep"), None)
    return jax.shard_map(
        on_device, mesh=mesh, in_specs=in_specs, out_specs=out_specs, check_vma=False
    )
```

```python
import jax
import jax.numpy as jnp
from jax import lax
from jax.experimental import pallas as pl
from jax.experimental.pallas import tpu as pltpu
from jax.sharding import PartitionSpec as P

CAP = 8
SEND_COLS = 1152
BACK_COLS = 1152
AROUND = (1, -1, 2)
VMEM_LIMIT = 48 * 1024 * 1024


def shifted(x, shift):
    n = lax.axis_size("dp")
    return lax.ppermute(x, "dp", [(i, (i + shift) % n) for i in range(n)])


def dot_f32(a, b):
    return jnp.dot(a, b, preferred_element_type=jnp.float32)


def split_hi_lo(x):
    hi = x.astype(jnp.bfloat16)
    lo = (x - hi.astype(jnp.float32)).astype(jnp.bfloat16)
    return hi, lo


def slot_codes(used):
    tok = used.shape[1]
    before = lax.broadcasted_iota(jnp.int32, (tok, tok), 0) < lax.broadcasted_iota(
        jnp.int32, (tok, tok), 1
    )
    ones = jnp.where(used, 1.0, 0.0)
    rank = dot_f32(
        ones.astype(jnp.bfloat16), jnp.where(before, 1.0, 0.0).astype(jnp.bfloat16)
    )
    return jnp.where(used, rank, -1.0)


def prepare_own(count, ids, weights, tokens, extended, send, hi_out, lo_out):
    top, tok = ids.shape
    feature = tokens.shape[1]
    n_experts = hi_out.shape[0] // CAP
    expert = lax.broadcasted_iota(jnp.int32, (n_experts, tok), 0)
    gates = jnp.zeros((n_experts, tok), jnp.float32)
    for k in range(top):
        gates = gates + jnp.where(expert == ids[k : k + 1, :], weights[k : k + 1, :], 0.0)
    live = lax.broadcasted_iota(jnp.int32, (n_experts, tok), 1) < count[0]
    gates = jnp.where(live, gates, 0.0)
    hi, lo = split_hi_lo(gates)
    code = slot_codes(gates > 0)
    want = lax.broadcasted_iota(jnp.int32, (n_experts, CAP, tok), 1).astype(jnp.float32)
    hit = code[:, None, :] == want
    shape = (n_experts * CAP, tok)
    one_hot = jnp.where(hit, 1.0, 0.0).reshape(shape).astype(jnp.bfloat16)
    spread = lambda g: jnp.where(hit, g.astype(jnp.float32)[:, None, :], 0.0).reshape(shape)
    hi_out[...] = spread(hi).astype(jnp.bfloat16)
    lo_out[...] = spread(lo).astype(jnp.bfloat16)
    extended[:, :feature] = tokens[...]
    extended[:, feature:] = jnp.concatenate(
        [hi.astype(jnp.float32), lo.astype(jnp.float32)], axis=1
    ).astype(jnp.bfloat16)
    step = 128
    for c in range(0, send.shape[1], step):
        send[:, c : c + step] = dot_f32(one_hot, tokens[:, c : c + step]).astype(jnp.bfloat16)


def prepare_ring(e0, e1, e2, e3, send, hi_out, lo_out, rows_out):
    tok, width = e0.shape
    feature = rows_out.shape[1]
    blocks = 4
    n_experts = hi_out.shape[0] // (blocks * CAP)
    first = feature - send.shape[1]
    parts = []
    his = []
    los = []
    for j, e in enumerate((e0, e1, e2, e3)):
        rows_out[j * tok : (j + 1) * tok, :] = e[:, :feature]
        meta = e[:, feature:].astype(jnp.float32)
        hi = meta[:, :tok]
        his.append(hi)
        los.append(meta[:, tok:])
        parts.append(slot_codes(hi > 0))
    code = jnp.concatenate(parts, axis=1)
    hi = jnp.concatenate(his, axis=1)
    lo = jnp.concatenate(los, axis=1)
    rows = blocks * tok
    chunk = 16
    shape = (chunk, blocks * CAP, rows)
    slot = lax.broadcasted_iota(jnp.int32, shape, 1)
    at = lax.broadcasted_iota(jnp.int32, shape, 2)
    want = jnp.where(at // tok == slot // CAP, slot % CAP, -2).astype(jnp.float32)
    flat = chunk * blocks * CAP
    for c in range(0, n_experts, chunk):
        hit = code[c : c + chunk, None, :] == want
        out = slice(c * blocks * CAP, c * blocks * CAP + flat)
        one_hot = jnp.where(hit, 1.0, 0.0).reshape(flat, rows).astype(jnp.bfloat16)
        spread = lambda g: (
            jnp.where(hit, g[c : c + chunk, None, :], 0.0).reshape(flat, rows).astype(jnp.bfloat16)
        )
        hi_out[out, :] = spread(hi)
        lo_out[out, :] = spread(lo)
        send[out, :] = dot_f32(one_hot, rows_out[:, first:]).astype(jnp.bfloat16)


def in_vmem(n):
    return [pl.BlockSpec(memory_space=pltpu.VMEM)] * n


def call_prepare_own(count, ids, weights, tokens, n_experts, cols):
    tok, feature = tokens.shape
    slots = n_experts * CAP
    return pl.pallas_call(
        prepare_own,
        in_specs=[pl.BlockSpec(memory_space=pltpu.SMEM)] + in_vmem(3),
        out_specs=in_vmem(4),
        out_shape=[
            jax.ShapeDtypeStruct((tok, feature + 2 * tok), jnp.bfloat16),
            jax.ShapeDtypeStruct((slots, cols), jnp.bfloat16),
            jax.ShapeDtypeStruct((slots, tok), jnp.bfloat16),
            jax.ShapeDtypeStruct((slots, tok), jnp.bfloat16),
        ],
        compiler_params=pltpu.CompilerParams(vmem_limit_bytes=VMEM_LIMIT),
        name="prepare_own",
    )(count, ids, weights, tokens)


def call_prepare_ring(around, n_experts, feature, cols):
    tok = around[0].shape[0]
    rows = len(around) * tok
    slots = n_experts * CAP * len(around)
    return pl.pallas_call(
        prepare_ring,
        in_specs=in_vmem(4),
        out_specs=in_vmem(4),
        out_shape=[
            jax.ShapeDtypeStruct((slots, cols), jnp.bfloat16),
            jax.ShapeDtypeStruct((slots, rows), jnp.bfloat16),
            jax.ShapeDtypeStruct((slots, rows), jnp.bfloat16),
            jax.ShapeDtypeStruct((rows, feature), jnp.bfloat16),
        ],
        compiler_params=pltpu.CompilerParams(vmem_limit_bytes=VMEM_LIMIT),
        name="prepare_ring",
    )(*around)


def expert_kernel(x0, x1, x2, x3, xb, wg, wu, wd, o0, o1, o2, o3, ob):
    dims = (((1,), (1,)), ((), ()))
    for j, (x, o) in enumerate(((x0, o0), (x1, o1), (x2, o2), (x3, o3))):
        cols = x.shape[-1]
        rows_d = x[0]
        rows_b = xb[0, j]

        def project(w):
            return lax.dot_general(
                rows_d, w[0, :, :cols], dims, preferred_element_type=jnp.float32
            ) + lax.dot_general(rows_b, w[0, :, cols:], dims, preferred_element_type=jnp.float32)

        gate = project(wg)
        up = project(wu)
        hidden = (gate / (1.0 + jnp.exp(-gate)) * up).astype(jnp.bfloat16)
        out = jnp.dot(hidden, wd[0], preferred_element_type=jnp.float32).astype(jnp.bfloat16)
        back = o.shape[-1]
        o[0] = out[:, :back]
        ob[0, j] = out[:, back:]


def run_experts(planes, xb, wg, wu, wd, back):
    members, rows, cols = planes[0].shape
    ffe, feature = wg.shape[1:]
    n = len(planes)
    one = lambda shape: pl.BlockSpec((1,) + shape, lambda m: (m,) + (0,) * len(shape))
    return pl.pallas_call(
        expert_kernel,
        grid=(members,),
        in_specs=[one((rows, cols))] * n
        + [one((n, rows, feature - cols))]
        + [one((ffe, feature))] * 3,
        out_specs=[one((rows, back))] * n + [one((n, rows, feature - back))],
        out_shape=[jax.ShapeDtypeStruct((members, rows, back), jnp.bfloat16)] * n
        + [jax.ShapeDtypeStruct((members, n, rows, feature - back), jnp.bfloat16)],
        compiler_params=pltpu.CompilerParams(vmem_limit_bytes=VMEM_LIMIT),
        cost_estimate=pl.CostEstimate(
            flops=members * n * rows * ffe * feature * 6,
            bytes_accessed=members * (n * rows * feature * 4 + 3 * ffe * feature * 2),
            transcendentals=members * n * rows * ffe,
        ),
        name="experts",
    )(*planes, xb, wg, wu, wd)


def weigh(hi, lo, values):
    contract = (((0,), (0,)), ((), ()))
    return lax.dot_general(
        hi, values, contract, preferred_element_type=jnp.float32
    ) + lax.dot_general(lo, values, contract, preferred_element_type=jnp.float32)


def on_device(
    tokens,
    row_counts,
    expert_ids,
    gate_weights,
    expert_gate,
    expert_up,
    expert_down,
    shared_gate,
    shared_up,
    shared_down,
):
    tok, feature = tokens.shape
    members = expert_gate.shape[0]
    n_ep = lax.axis_size("ep")
    n_dp = lax.axis_size("dp")
    n_experts = members * n_ep
    sc, bc = SEND_COLS, BACK_COLS

    def over_ep(x, rows, cols):
        return lax.all_to_all(
            x.reshape(n_ep, rows, cols), "ep", split_axis=0, concat_axis=0, tiled=True
        )

    extended, send_d, hi_d, lo_d = call_prepare_own(
        row_counts, expert_ids.T, gate_weights.T, tokens, n_experts, sc
    )
    came_d = over_ep(send_d, members * CAP, sc)

    around = [extended] + [shifted(extended, s) for s in AROUND]
    send_b, hi_b, lo_b, gathered = call_prepare_ring(around, n_experts, feature, feature - sc)

    own = (
        came_d.reshape(n_ep, members, CAP, sc)
        .transpose(1, 0, 2, 3)
        .reshape(members, n_ep * CAP, sc)
    )
    planes = [own] + [shifted(own, s) for s in AROUND]
    came_b = over_ep(send_b, members * n_dp * CAP, feature - sc)
    xb = (
        came_b.reshape(n_ep, members, n_dp, CAP, feature - sc)
        .transpose(1, 2, 0, 3, 4)
        .reshape(members, n_dp, n_ep * CAP, feature - sc)
    )

    gate_act = dot_f32(gathered, shared_gate)
    up_act = dot_f32(gathered, shared_up)
    hidden = (jax.nn.silu(gate_act) * up_act).astype(jnp.bfloat16)
    shared = dot_f32(hidden, shared_down)
    planes[0], shared = lax.optimization_barrier((planes[0], shared))

    *out_d, out_b = run_experts(
        planes,
        xb,
        expert_gate.swapaxes(1, 2),
        expert_up.swapaxes(1, 2),
        expert_down,
        bc,
    )
    back_b = out_b.reshape(members, n_dp, n_ep, CAP, feature - bc).transpose(2, 0, 1, 3, 4)
    ret_b = over_ep(back_b, members * n_dp * CAP, feature - bc)

    total_d = out_d[0].astype(jnp.float32)
    for j, s in enumerate(AROUND):
        total_d = total_d + shifted(out_d[j + 1], -s).astype(jnp.float32)
    back_d = (
        total_d.astype(jnp.bfloat16).reshape(members, n_ep, CAP, bc).transpose(1, 0, 2, 3)
    )
    back_d, ret_b = lax.optimization_barrier((back_d, ret_b))
    ret_d = over_ep(back_d, members * CAP, bc)

    routed_b = weigh(hi_b, lo_b, ret_b.reshape(-1, feature - bc))
    partial_sum = jnp.concatenate(
        [shared[:, :bc], shared[:, bc:] + routed_b], axis=1
    ).astype(jnp.bfloat16)
    total = partial_sum[:tok].astype(jnp.float32)
    for j, s in enumerate(AROUND):
        part = partial_sum[(j + 1) * tok : (j + 2) * tok]
        total = total + shifted(part, -s).astype(jnp.float32)

    routed_d = weigh(hi_d, lo_d, ret_d.reshape(-1, bc))
    result = total + jnp.concatenate(
        [routed_d, jnp.zeros((tok, feature - bc), jnp.float32)], axis=1
    )
    live = jnp.arange(tok, dtype=jnp.int32) < row_counts[0]
    return jnp.where(live[:, None], result, 0.0).astype(jnp.bfloat16)


def solution(mesh):
    in_specs = (
        P(("dp", "ep"), None),
        P(("dp", "ep")),
        P(("dp", "ep"), None),
        P(("dp", "ep"), None),
        P("ep", None, "dp"),
        P("ep", None, "dp"),
        P("ep", "dp", None),
        P(None, "dp"),
        P(None, "dp"),
        P("dp", None),
    )
    out_specs = P(("dp", "ep"), None)
    return jax.shard_map(
        on_device, mesh=mesh, in_specs=in_specs, out_specs=out_specs, check_vma=False
    )
```

```python
import functools

import jax
import jax.numpy as jnp
from jax import lax
from jax.experimental import pallas as pl
from jax.experimental.pallas import tpu as pltpu
from jax.sharding import PartitionSpec as P

CAP = 8
SEND_COLS = 1280
BACK_COLS = 1280
COLS = 128
NT = (((1,), (1,)), ((), ()))
TN = (((0,), (0,)), ((), ()))
AROUND = (2, 1, -1)
VMEM_LIMIT = 48 * 1024 * 1024


def shifted(x, shift):
    n = lax.axis_size("dp")
    return lax.ppermute(x, "dp", [(i, (i + shift) % n) for i in range(n)])


def dot_f32(a, b):
    return jnp.dot(a, b, preferred_element_type=jnp.float32)


def split_hi_lo(x):
    hi = x.astype(jnp.bfloat16)
    lo = (x - hi.astype(jnp.float32)).astype(jnp.bfloat16)
    return hi, lo


def slot_codes(used):
    tok = used.shape[1]
    before = lax.broadcasted_iota(jnp.int32, (tok, tok), 0) < lax.broadcasted_iota(
        jnp.int32, (tok, tok), 1
    )
    ones = jnp.where(used, 1.0, 0.0)
    rank = dot_f32(
        ones.astype(jnp.bfloat16), jnp.where(before, 1.0, 0.0).astype(jnp.bfloat16)
    )
    return jnp.where(used, rank, -1.0)


def prepare_own(count, ids, weights, tokens, extended, send, hi_out, lo_out):
    top, tok = ids.shape
    feature = tokens.shape[1]
    n_experts = hi_out.shape[0] // CAP
    expert = lax.broadcasted_iota(jnp.int32, (n_experts, tok), 0)
    gates = jnp.zeros((n_experts, tok), jnp.float32)
    for k in range(top):
        gates = gates + jnp.where(expert == ids[k : k + 1, :], weights[k : k + 1, :], 0.0)
    live = lax.broadcasted_iota(jnp.int32, (n_experts, tok), 1) < count[0]
    gates = jnp.where(live, gates, 0.0)
    hi, lo = split_hi_lo(gates)
    code = slot_codes(gates > 0)
    want = lax.broadcasted_iota(jnp.int32, (n_experts, CAP, tok), 1).astype(jnp.float32)
    hit = code[:, None, :] == want
    shape = (n_experts * CAP, tok)
    one_hot = jnp.where(hit, 1.0, 0.0).reshape(shape).astype(jnp.bfloat16)
    spread = lambda g: jnp.where(hit, g.astype(jnp.float32)[:, None, :], 0.0).reshape(shape)
    hi_out[...] = spread(hi).astype(jnp.bfloat16)
    lo_out[...] = spread(lo).astype(jnp.bfloat16)
    extended[:, :feature] = tokens[...]
    extended[:, feature:] = jnp.concatenate(
        [hi.astype(jnp.float32), lo.astype(jnp.float32)], axis=1
    ).astype(jnp.bfloat16)
    step = 128
    for c in range(0, send.shape[1], step):
        send[:, c : c + step] = dot_f32(one_hot, tokens[:, c : c + step]).astype(jnp.bfloat16)


def prepare_ring(e0, e1, e2, e3, send, hi_out, lo_out, rows_out):
    tok, width = e0.shape
    feature = rows_out.shape[1]
    blocks = 4
    n_experts = hi_out.shape[0] // (blocks * CAP)
    first = feature - send.shape[1]
    parts = []
    his = []
    los = []
    for j, e in enumerate((e0, e1, e2, e3)):
        rows_out[j * tok : (j + 1) * tok, :] = e[:, :feature]
        meta = e[:, feature:].astype(jnp.float32)
        hi = meta[:, :tok]
        his.append(hi)
        los.append(meta[:, tok:])
        parts.append(slot_codes(hi > 0))
    code = jnp.concatenate(parts, axis=1)
    hi = jnp.concatenate(his, axis=1)
    lo = jnp.concatenate(los, axis=1)
    rows = blocks * tok
    chunk = 16
    shape = (chunk, blocks * CAP, rows)
    slot = lax.broadcasted_iota(jnp.int32, shape, 1)
    at = lax.broadcasted_iota(jnp.int32, shape, 2)
    want = jnp.where(at // tok == slot // CAP, slot % CAP, -2).astype(jnp.float32)
    flat = chunk * blocks * CAP
    for c in range(0, n_experts, chunk):
        hit = code[c : c + chunk, None, :] == want
        out = slice(c * blocks * CAP, c * blocks * CAP + flat)
        one_hot = jnp.where(hit, 1.0, 0.0).reshape(flat, rows).astype(jnp.bfloat16)
        spread = lambda g: (
            jnp.where(hit, g[c : c + chunk, None, :], 0.0).reshape(flat, rows).astype(jnp.bfloat16)
        )
        hi_out[out, :] = spread(hi)
        lo_out[out, :] = spread(lo)
        send[out, :] = dot_f32(one_hot, rows_out[:, first:]).astype(jnp.bfloat16)


def in_vmem(n):
    return [pl.BlockSpec(memory_space=pltpu.VMEM)] * n


def call_prepare_own(count, ids, weights, tokens, n_experts, cols):
    tok, feature = tokens.shape
    slots = n_experts * CAP
    return pl.pallas_call(
        prepare_own,
        in_specs=[pl.BlockSpec(memory_space=pltpu.SMEM)] + in_vmem(3),
        out_specs=in_vmem(4),
        out_shape=[
            jax.ShapeDtypeStruct((tok, feature + 2 * tok), jnp.bfloat16),
            jax.ShapeDtypeStruct((slots, cols), jnp.bfloat16),
            jax.ShapeDtypeStruct((slots, tok), jnp.bfloat16),
            jax.ShapeDtypeStruct((slots, tok), jnp.bfloat16),
        ],
        compiler_params=pltpu.CompilerParams(vmem_limit_bytes=VMEM_LIMIT),
        name="prepare_own",
    )(count, ids, weights, tokens)


def call_prepare_ring(around, n_experts, feature, cols):
    tok = around[0].shape[0]
    rows = len(around) * tok
    slots = n_experts * CAP * len(around)
    return pl.pallas_call(
        prepare_ring,
        in_specs=in_vmem(4),
        out_specs=in_vmem(4),
        out_shape=[
            jax.ShapeDtypeStruct((slots, cols), jnp.bfloat16),
            jax.ShapeDtypeStruct((slots, rows), jnp.bfloat16),
            jax.ShapeDtypeStruct((slots, rows), jnp.bfloat16),
            jax.ShapeDtypeStruct((rows, feature), jnp.bfloat16),
        ],
        compiler_params=pltpu.CompilerParams(vmem_limit_bytes=VMEM_LIMIT),
        name="prepare_ring",
    )(*around)


def expert_kernel(splits, *refs):
    n_x = sum(len(s) for s in splits)
    xin, (xb, wg, wu, wd) = refs[:n_x], refs[n_x : n_x + 4]
    rest = refs[n_x + 4 :]
    rest = rest[len(rest) - (n_x + 3) :]
    outs, (ob, xs, keep) = rest[:n_x], rest[n_x:]
    member = pl.program_id(0)
    sc, bc = xin[0].shape[-1], outs[0].shape[-1]
    feature = wg.shape[2]
    n_ep, slots = xb.shape[:2]
    rows = n_ep * CAP
    planes = len(splits)
    at = 0
    place = []
    for p, split in enumerate(splits):
        row = p * rows
        for n in split:
            place.append((xin[at], outs[at], row, n))
            row += n * CAP
            at += 1
    for x, _, row, n in place:
        for c in range(0, sc, COLS):
            part = x[:, :, c : c + COLS].astype(jnp.float32).reshape(n, 2, CAP, COLS)
            part = jnp.where(member == 0, part[:, 0], part[:, 1])
            xs[row : row + n * CAP, c : c + COLS] = part.reshape(n * CAP, COLS).astype(jnp.bfloat16)
    for c in range(0, feature - sc, COLS):
        part = xb[:, :, c : c + COLS].astype(jnp.float32).reshape(n_ep, planes, CAP, COLS)
        for p in range(planes):
            xs[p * rows : (p + 1) * rows, sc + c : sc + c + COLS] = (
                part[:, p].reshape(rows, COLS).astype(jnp.bfloat16)
            )
    gate = lax.dot_general(wg[0], xs[...], NT, preferred_element_type=jnp.float32)
    up = lax.dot_general(wu[0], xs[...], NT, preferred_element_type=jnp.float32)
    hidden = (gate / (1.0 + jnp.exp(-gate)) * up).astype(jnp.bfloat16)
    out = lax.dot_general(hidden, wd[0], TN, preferred_element_type=jnp.float32)
    for c in range(0, feature - bc, COLS):
        part = out[:, bc + c : bc + c + COLS].reshape(planes, n_ep, CAP, COLS)
        part = jnp.stack([part[p] for p in range(planes)], axis=1)
        ob[:, :, c : c + COLS] = part.reshape(n_ep, slots, COLS).astype(jnp.bfloat16)

    @pl.when(member == 0)
    def _():
        keep[...] = out[:, :bc]

    @pl.when(member == 1)
    def _():
        for _, o, row, n in place:
            for c in range(0, bc, COLS):
                parts = [
                    keep[row : row + n * CAP, c : c + COLS].reshape(n, CAP, COLS),
                    out[row : row + n * CAP, c : c + COLS].reshape(n, CAP, COLS),
                ]
                o[:, :, c : c + COLS] = (
                    jnp.stack(parts, axis=1).reshape(n, 2 * CAP, COLS).astype(jnp.bfloat16)
                )


def run_experts(planes, pair, xb, sofar, wg, wu, wd, back):
    members, ffe, feature = wg.shape
    xin = [x for plane in planes for x in plane]
    splits = tuple(tuple(x.shape[0] for x in plane) for plane in planes)
    n_ep, slots, cols_b = xb.shape
    step = len(planes) * CAP
    pairs = slots // (members * step)
    rows = len(planes) * n_ep * CAP
    whole = lambda shape: pl.BlockSpec(shape, lambda m: (0,) * len(shape))
    one = lambda shape: pl.BlockSpec((1,) + shape, lambda m: (m,) + (0,) * len(shape))
    slot = lambda cols: pl.BlockSpec((n_ep, step, cols), lambda m: (0, m * pairs + pair, 0))
    out_x = [jax.ShapeDtypeStruct(x.shape[:2] + (back,), jnp.bfloat16) for x in xin]
    operands = [*xin, xb, wg, wu, wd]
    in_specs = [whole(x.shape) for x in xin] + [slot(cols_b)] + [one((ffe, feature))] * 3
    aliases = {}
    if sofar is not None:
        aliases = {len(operands): len(xin)}
        operands.append(sofar)
        in_specs.append(pl.BlockSpec(memory_space=pl.ANY))
    return pl.pallas_call(
        functools.partial(expert_kernel, splits),
        grid=(members,),
        in_specs=in_specs,
        out_specs=[whole(x.shape) for x in out_x] + [slot(feature - back)],
        out_shape=out_x + [jax.ShapeDtypeStruct((n_ep, slots, feature - back), jnp.bfloat16)],
        scratch_shapes=[
            pltpu.VMEM((rows, feature), jnp.bfloat16),
            pltpu.VMEM((rows, back), jnp.float32),
        ],
        input_output_aliases=aliases,
        compiler_params=pltpu.CompilerParams(vmem_limit_bytes=VMEM_LIMIT),
        cost_estimate=pl.CostEstimate(
            flops=members * rows * ffe * feature * 6,
            bytes_accessed=members * (rows * feature * 4 + 3 * ffe * feature * 2),
            transcendentals=members * rows * ffe,
        ),
        name="experts",
    )(*operands)


def weigh(hi, lo, values):
    return lax.dot_general(hi, values, TN, preferred_element_type=jnp.float32) + lax.dot_general(
        lo, values, TN, preferred_element_type=jnp.float32
    )


def on_device(
    tokens,
    row_counts,
    expert_ids,
    gate_weights,
    expert_gate,
    expert_up,
    expert_down,
    shared_gate,
    shared_up,
    shared_down,
):
    tok, feature = tokens.shape
    members = expert_gate.shape[0]
    n_ep = lax.axis_size("ep")
    n_dp = lax.axis_size("dp")
    n_experts = members * n_ep
    sc, bc = SEND_COLS, BACK_COLS

    def over_ep(x, rows, cols):
        return lax.all_to_all(
            x.reshape(n_ep, rows, cols), "ep", split_axis=0, concat_axis=0, tiled=True
        )

    extended, send_d, hi_d, lo_d = call_prepare_own(
        row_counts, expert_ids.T, gate_weights.T, tokens, n_experts, sc
    )
    own = over_ep(send_d, members * CAP, sc)

    around = [shifted(extended, s) for s in AROUND] + [extended]
    send_b, hi_b, lo_b, gathered = call_prepare_ring(around, n_experts, feature, feature - sc)

    half = n_ep // 2
    below, above = shifted(own, 1), shifted(own, -1)
    far = [shifted(below[:half], 1), shifted(above[half:], -1)]
    came_b = over_ep(send_b, members * n_dp * CAP, feature - sc)

    gate_act = dot_f32(gathered, shared_gate)
    up_act = dot_f32(gathered, shared_up)
    hidden = (jax.nn.silu(gate_act) * up_act).astype(jnp.bfloat16)
    shared = dot_f32(hidden, shared_down)
    came_b, shared = lax.optimization_barrier((came_b, shared))

    weights = (expert_gate.swapaxes(1, 2), expert_up.swapaxes(1, 2), expert_down)
    far_0, far_1, to_below, out_b = run_experts([far, [below]], 0, came_b, None, *weights, bc)
    to_above, total_d, out_b = run_experts([[above], [own]], 1, came_b, out_b, *weights, bc)
    ret_b = over_ep(out_b, members * n_dp * CAP, feature - bc)

    f32 = lambda x: x.astype(jnp.float32)
    from_below, from_above = shifted(far_0, 1), shifted(far_1, -1)
    to_above = jnp.concatenate(
        [(f32(to_above[:half]) + f32(from_below)).astype(jnp.bfloat16), to_above[half:]]
    )
    to_below = jnp.concatenate(
        [to_below[:half], (f32(to_below[half:]) + f32(from_above)).astype(jnp.bfloat16)]
    )
    back_d = (
        f32(total_d) + f32(shifted(to_above, 1)) + f32(shifted(to_below, -1))
    ).astype(jnp.bfloat16)
    back_d, ret_b = lax.optimization_barrier((back_d, ret_b))
    ret_d = over_ep(back_d, members * CAP, bc)

    routed_b = weigh(hi_b, lo_b, ret_b.reshape(-1, feature - bc))
    partial_sum = jnp.concatenate(
        [shared[:, :bc], shared[:, bc:] + routed_b], axis=1
    ).astype(jnp.bfloat16)
    total = partial_sum[len(AROUND) * tok :].astype(jnp.float32)
    for j, s in enumerate(AROUND):
        part = partial_sum[j * tok : (j + 1) * tok]
        total = total + shifted(part, -s).astype(jnp.float32)

    routed_d = weigh(hi_d, lo_d, ret_d.reshape(-1, bc))
    result = total + jnp.concatenate(
        [routed_d, jnp.zeros((tok, feature - bc), jnp.float32)], axis=1
    )
    live = jnp.arange(tok, dtype=jnp.int32) < row_counts[0]
    return jnp.where(live[:, None], result, 0.0).astype(jnp.bfloat16)


def solution(mesh):
    in_specs = (
        P(("dp", "ep"), None),
        P(("dp", "ep")),
        P(("dp", "ep"), None),
        P(("dp", "ep"), None),
        P("ep", None, "dp"),
        P("ep", None, "dp"),
        P("ep", "dp", None),
        P(None, "dp"),
        P(None, "dp"),
        P("dp", None),
    )
    out_specs = P(("dp", "ep"), None)
    return jax.shard_map(
        on_device, mesh=mesh, in_specs=in_specs, out_specs=out_specs, check_vma=False
    )
```

```python
import functools

import jax
import jax.numpy as jnp
from jax import lax
from jax.experimental import pallas as pl
from jax.experimental.pallas import tpu as pltpu
from jax.sharding import PartitionSpec as P

CAP = 8
SEND_COLS = 1280
BACK_COLS = 1280
COLS = 128
NT = (((1,), (1,)), ((), ()))
TN = (((0,), (0,)), ((), ()))
AROUND = (2, 1, -1)
VMEM_LIMIT = 40 * 1024 * 1024


def shifted(x, shift):
    n = lax.axis_size("dp")
    return lax.ppermute(x, "dp", [(i, (i + shift) % n) for i in range(n)])


def toward(x):
    n, m = lax.axis_size("dp"), lax.axis_size("ep")
    pairs = []
    for i in range(n):
        for e in range(m):
            step = 1 if e % 2 == 0 else -1
            pairs.append((i * m + e, (i + step) % n * m + e))
    return lax.ppermute(x, ("dp", "ep"), pairs)


def dot_f32(a, b):
    return jnp.dot(a, b, preferred_element_type=jnp.float32)


def split_hi_lo(x):
    hi = x.astype(jnp.bfloat16)
    lo = (x - hi.astype(jnp.float32)).astype(jnp.bfloat16)
    return hi, lo


def slot_codes(used):
    tok = used.shape[1]
    before = lax.broadcasted_iota(jnp.int32, (tok, tok), 0) < lax.broadcasted_iota(
        jnp.int32, (tok, tok), 1
    )
    ones = jnp.where(used, 1.0, 0.0)
    rank = dot_f32(
        ones.astype(jnp.bfloat16), jnp.where(before, 1.0, 0.0).astype(jnp.bfloat16)
    )
    return jnp.where(used, rank, -1.0)


def prepare_own(count, ids, weights, tokens, extended, send, hi_out, lo_out):
    top, tok = ids.shape
    feature = tokens.shape[1]
    n_experts = hi_out.shape[0] // CAP
    expert = lax.broadcasted_iota(jnp.int32, (n_experts, tok), 0)
    gates = jnp.zeros((n_experts, tok), jnp.float32)
    for k in range(top):
        gates = gates + jnp.where(expert == ids[k : k + 1, :], weights[k : k + 1, :], 0.0)
    live = lax.broadcasted_iota(jnp.int32, (n_experts, tok), 1) < count[0]
    gates = jnp.where(live, gates, 0.0)
    hi, lo = split_hi_lo(gates)
    code = slot_codes(gates > 0)
    want = lax.broadcasted_iota(jnp.int32, (n_experts, CAP, tok), 1).astype(jnp.float32)
    hit = code[:, None, :] == want
    shape = (n_experts * CAP, tok)
    one_hot = jnp.where(hit, 1.0, 0.0).reshape(shape).astype(jnp.bfloat16)
    spread = lambda g: jnp.where(hit, g.astype(jnp.float32)[:, None, :], 0.0).reshape(shape)
    hi_out[...] = spread(hi).astype(jnp.bfloat16)
    lo_out[...] = spread(lo).astype(jnp.bfloat16)
    extended[:, :feature] = tokens[...]
    extended[:, feature:] = jnp.concatenate(
        [hi.astype(jnp.float32), lo.astype(jnp.float32)], axis=1
    ).astype(jnp.bfloat16)
    step = 128
    for c in range(0, send.shape[1], step):
        send[:, c : c + step] = dot_f32(one_hot, tokens[:, c : c + step]).astype(jnp.bfloat16)


def prepare_ring(members, e0, e1, e2, e3, send, hi_out, lo_out, rows_out):
    tok, width = e0.shape
    feature = rows_out.shape[1]
    blocks = 4
    n_experts = hi_out.shape[0] // (blocks * CAP)
    first = feature - send.shape[1]
    parts = []
    his = []
    los = []
    for j, e in enumerate((e0, e1, e2, e3)):
        rows_out[j * tok : (j + 1) * tok, :] = e[:, :feature]
        meta = e[:, feature:].astype(jnp.float32)
        hi = meta[:, :tok]
        his.append(hi)
        los.append(meta[:, tok:])
        parts.append(slot_codes(hi > 0))
    code = jnp.concatenate(parts, axis=1)
    hi = jnp.concatenate(his, axis=1)
    lo = jnp.concatenate(los, axis=1)
    rows = blocks * tok
    chunk = 16
    shape = (chunk, blocks * CAP, rows)
    slot = lax.broadcasted_iota(jnp.int32, shape, 1)
    at = lax.broadcasted_iota(jnp.int32, shape, 2)
    block = slot // CAP
    odd = lax.broadcasted_iota(jnp.int32, shape, 0) // members % 2 == 1
    block = jnp.where(odd & (block == 1), 2, jnp.where(odd & (block == 2), 1, block))
    want = jnp.where(at // tok == block, slot % CAP, -2).astype(jnp.float32)
    flat = chunk * blocks * CAP
    for c in range(0, n_experts, chunk):
        hit = code[c : c + chunk, None, :] == want
        out = slice(c * blocks * CAP, c * blocks * CAP + flat)
        one_hot = jnp.where(hit, 1.0, 0.0).reshape(flat, rows).astype(jnp.bfloat16)
        spread = lambda g: (
            jnp.where(hit, g[c : c + chunk, None, :], 0.0).reshape(flat, rows).astype(jnp.bfloat16)
        )
        hi_out[out, :] = spread(hi)
        lo_out[out, :] = spread(lo)
        send[out, :] = dot_f32(one_hot, rows_out[:, first:]).astype(jnp.bfloat16)


def call_prepare_own(count, ids, weights, tokens, n_experts, cols):
    tok, feature = tokens.shape
    slots = n_experts * CAP
    return pl.pallas_call(
        prepare_own,
        in_specs=[pl.BlockSpec(memory_space=pltpu.SMEM)] + [pl.BlockSpec()] * 3,
        out_shape=[
            jax.ShapeDtypeStruct((tok, feature + 2 * tok), jnp.bfloat16),
            jax.ShapeDtypeStruct((slots, cols), jnp.bfloat16),
            jax.ShapeDtypeStruct((slots, tok), jnp.bfloat16),
            jax.ShapeDtypeStruct((slots, tok), jnp.bfloat16),
        ],
        compiler_params=pltpu.CompilerParams(vmem_limit_bytes=24 * 1024 * 1024),
        name="prepare_own",
    )(count, ids, weights, tokens)


def call_prepare_ring(around, members, n_experts, feature, cols):
    tok = around[0].shape[0]
    rows = len(around) * tok
    slots = n_experts * CAP * len(around)
    return pl.pallas_call(
        functools.partial(prepare_ring, members),
        out_shape=[
            jax.ShapeDtypeStruct((slots, cols), jnp.bfloat16),
            jax.ShapeDtypeStruct((slots, rows), jnp.bfloat16),
            jax.ShapeDtypeStruct((slots, rows), jnp.bfloat16),
            jax.ShapeDtypeStruct((rows, feature), jnp.bfloat16),
        ],
        compiler_params=pltpu.CompilerParams(vmem_limit_bytes=24 * 1024 * 1024),
        name="prepare_ring",
    )(*around)


def expert_kernel(splits, *refs):
    n_x = sum(len(s) for s in splits)
    xin, (xb, wg, wu, wd) = refs[:n_x], refs[n_x : n_x + 4]
    rest = refs[n_x + 4 :]
    rest = rest[len(rest) - (n_x + 3) :]
    outs, (ob, xs, keep) = rest[:n_x], rest[n_x:]
    member = pl.program_id(0)
    sc, bc = xin[0].shape[-1], outs[0].shape[-1]
    feature = wg.shape[2]
    n_ep, slots = xb.shape[:2]
    rows = n_ep * CAP
    planes = len(splits)
    at = 0
    place = []
    for p, split in enumerate(splits):
        row = p * rows
        for n in split:
            place.append((xin[at], outs[at], row, n))
            row += n * CAP
            at += 1
    for x, _, row, n in place:
        for c in range(0, sc, COLS):
            part = x[:, :, c : c + COLS].astype(jnp.float32).reshape(n, 2, CAP, COLS)
            part = jnp.where(member == 0, part[:, 0], part[:, 1])
            xs[row : row + n * CAP, c : c + COLS] = part.reshape(n * CAP, COLS).astype(jnp.bfloat16)
    for c in range(0, feature - sc, COLS):
        part = xb[:, :, c : c + COLS].astype(jnp.float32).reshape(n_ep, planes, CAP, COLS)
        for p in range(planes):
            xs[p * rows : (p + 1) * rows, sc + c : sc + c + COLS] = (
                part[:, p].reshape(rows, COLS).astype(jnp.bfloat16)
            )
    gate = lax.dot_general(wg[0], xs[...], NT, preferred_element_type=jnp.float32)
    up = lax.dot_general(wu[0], xs[...], NT, preferred_element_type=jnp.float32)
    hidden = (gate / (1.0 + jnp.exp(-gate)) * up).astype(jnp.bfloat16)
    out = lax.dot_general(hidden, wd[0], TN, preferred_element_type=jnp.float32)
    for c in range(0, feature - bc, COLS):
        part = out[:, bc + c : bc + c + COLS].reshape(planes, n_ep, CAP, COLS)
        part = jnp.stack([part[p] for p in range(planes)], axis=1)
        ob[:, :, c : c + COLS] = part.reshape(n_ep, slots, COLS).astype(jnp.bfloat16)

    @pl.when(member == 0)
    def _():
        keep[...] = out[:, :bc]

    @pl.when(member == 1)
    def _():
        for _, o, row, n in place:
            for c in range(0, bc, COLS):
                parts = [
                    keep[row : row + n * CAP, c : c + COLS].reshape(n, CAP, COLS),
                    out[row : row + n * CAP, c : c + COLS].reshape(n, CAP, COLS),
                ]
                o[:, :, c : c + COLS] = (
                    jnp.stack(parts, axis=1).reshape(n, 2 * CAP, COLS).astype(jnp.bfloat16)
                )


def run_experts(planes, pair, xb, sofar, wg, wu, wd, back):
    members, ffe, feature = wg.shape
    xin = [x for plane in planes for x in plane]
    splits = tuple(tuple(x.shape[0] for x in plane) for plane in planes)
    n_ep, slots, cols_b = xb.shape
    step = len(planes) * CAP
    pairs = slots // (members * step)
    rows = len(planes) * n_ep * CAP
    whole = lambda shape: pl.BlockSpec(shape, lambda m: (0,) * len(shape))
    one = lambda shape: pl.BlockSpec((1,) + shape, lambda m: (m,) + (0,) * len(shape))
    slot = lambda cols: pl.BlockSpec((n_ep, step, cols), lambda m: (0, m * pairs + pair, 0))
    out_x = [jax.ShapeDtypeStruct(x.shape[:2] + (back,), jnp.bfloat16) for x in xin]
    operands = [*xin, xb, wg, wu, wd]
    in_specs = [whole(x.shape) for x in xin] + [slot(cols_b)] + [one((ffe, feature))] * 3
    aliases = {}
    if sofar is not None:
        aliases = {len(operands): len(xin)}
        operands.append(sofar)
        in_specs.append(pl.BlockSpec(memory_space=pl.ANY))
    return pl.pallas_call(
        functools.partial(expert_kernel, splits),
        grid=(members,),
        in_specs=in_specs,
        out_specs=[whole(x.shape) for x in out_x] + [slot(feature - back)],
        out_shape=out_x + [jax.ShapeDtypeStruct((n_ep, slots, feature - back), jnp.bfloat16)],
        scratch_shapes=[
            pltpu.VMEM((rows, feature), jnp.bfloat16),
            pltpu.VMEM((rows, back), jnp.float32),
        ],
        input_output_aliases=aliases,
        compiler_params=pltpu.CompilerParams(vmem_limit_bytes=VMEM_LIMIT),
        cost_estimate=pl.CostEstimate(
            flops=members * rows * ffe * feature * 6,
            bytes_accessed=members * (rows * feature * 4 + 3 * ffe * feature * 2),
            transcendentals=members * rows * ffe,
        ),
        name="experts",
    )(*operands)


def weigh(hi, lo, values):
    return lax.dot_general(hi, values, TN, preferred_element_type=jnp.float32) + lax.dot_general(
        lo, values, TN, preferred_element_type=jnp.float32
    )


def combine(hi, lo, values, shared, *outs):
    tok, feature = outs[0].shape
    bc = feature - values.shape[1]
    for c in range(0, feature, 2 * COLS):
        cols = slice(c, c + 2 * COLS)
        total = shared[:, cols]
        if c >= bc:
            total = total + weigh(hi[...], lo[...], values[:, c - bc : c - bc + 2 * COLS])
        for j, o in enumerate(outs):
            o[:, cols] = total[j * tok : (j + 1) * tok].astype(jnp.bfloat16)


def call_combine(hi, lo, values, shared, tok):
    rows, feature = shared.shape
    return pl.pallas_call(
        combine,
        out_shape=[jax.ShapeDtypeStruct((tok, feature), jnp.bfloat16)] * (rows // tok),
        compiler_params=pltpu.CompilerParams(vmem_limit_bytes=24 * 1024 * 1024),
        name="combine",
    )(hi, lo, values, shared)


def finish(hi, lo, values, total, out):
    bc = values.shape[1]
    out[:, bc:] = total[:, bc:].astype(jnp.bfloat16)
    for c in range(0, bc, 2 * COLS):
        cols = slice(c, c + 2 * COLS)
        out[:, cols] = (total[:, cols] + weigh(hi[...], lo[...], values[:, cols])).astype(
            jnp.bfloat16
        )


def call_finish(hi, lo, values, total):
    return pl.pallas_call(
        finish,
        out_shape=jax.ShapeDtypeStruct(total.shape, jnp.bfloat16),
        compiler_params=pltpu.CompilerParams(vmem_limit_bytes=16 * 1024 * 1024),
        name="finish",
    )(hi, lo, values, total)


def on_device(
    tokens,
    row_counts,
    expert_ids,
    gate_weights,
    expert_gate,
    expert_up,
    expert_down,
    shared_gate,
    shared_up,
    shared_down,
):
    tok, feature = tokens.shape
    members = expert_gate.shape[0]
    n_ep = lax.axis_size("ep")
    n_dp = lax.axis_size("dp")
    n_experts = members * n_ep
    sc, bc = SEND_COLS, BACK_COLS

    def over_ep(x, rows, cols):
        return lax.all_to_all(
            x.reshape(n_ep, rows, cols), "ep", split_axis=0, concat_axis=0, tiled=True
        )

    extended, send_d, hi_d, lo_d = call_prepare_own(
        row_counts, expert_ids.T, gate_weights.T, tokens, n_experts, sc
    )
    own = over_ep(send_d, members * CAP, sc)

    around = [shifted(extended, s) for s in AROUND] + [extended]
    send_b, hi_b, lo_b, gathered = call_prepare_ring(
        around, members, n_experts, feature, feature - sc
    )

    half = n_ep // 2
    own_parts = [own[:half], own[half:]]
    behind = [toward(x) for x in own_parts]
    far = [toward(x) for x in behind]
    ahead = [toward(x) for x in far]
    came_b = over_ep(send_b, members * n_dp * CAP, feature - sc)

    gate_act = dot_f32(gathered, shared_gate)
    up_act = dot_f32(gathered, shared_up)
    hidden = (jax.nn.silu(gate_act) * up_act).astype(jnp.bfloat16)
    shared = dot_f32(hidden, shared_down)
    came_b, shared = lax.optimization_barrier((came_b, shared))

    weights = (expert_gate.swapaxes(1, 2), expert_up.swapaxes(1, 2), expert_down)
    f0, f1, b0, b1, out_b = run_experts([far, behind], 0, came_b, None, *weights, bc)
    a0, a1, o0, o1, out_b = run_experts([ahead, own_parts], 1, came_b, out_b, *weights, bc)
    ret_b = over_ep(out_b, members * n_dp * CAP, feature - bc)

    f32 = lambda x: x.astype(jnp.float32)
    ends = []
    for first, second, third, last in ((b0, f0, a0, o0), (b1, f1, a1, o1)):
        passing = first
        for mine in (second, third):
            passing = (f32(mine) + f32(toward(passing))).astype(jnp.bfloat16)
        ends.append((f32(last) + f32(toward(passing))).astype(jnp.bfloat16))
    back_d = jnp.concatenate(ends)
    back_d, ret_b = lax.optimization_barrier((back_d, ret_b))
    ret_d = over_ep(back_d, members * CAP, bc)

    *parts, kept = call_combine(hi_b, lo_b, ret_b.reshape(-1, feature - bc), shared, tok)
    live = jnp.arange(tok, dtype=jnp.int32) < row_counts[0]
    total = f32(kept)
    for part, s in zip(parts, AROUND):
        total = total + f32(shifted(part, -s))
    total = jnp.where(live[:, None], total, 0.0)
    return call_finish(hi_d, lo_d, ret_d.reshape(-1, bc), total)


def solution(mesh):
    in_specs = (
        P(("dp", "ep"), None),
        P(("dp", "ep")),
        P(("dp", "ep"), None),
        P(("dp", "ep"), None),
        P("ep", None, "dp"),
        P("ep", None, "dp"),
        P("ep", "dp", None),
        P(None, "dp"),
        P(None, "dp"),
        P("dp", None),
    )
    out_specs = P(("dp", "ep"), None)
    return jax.shard_map(
        on_device, mesh=mesh, in_specs=in_specs, out_specs=out_specs, check_vma=False
    )
```

```python
import functools

import jax
import jax.numpy as jnp
from jax import lax
from jax.experimental import pallas as pl
from jax.experimental.pallas import tpu as pltpu
from jax.sharding import PartitionSpec as P

CAP = 8
SEND_COLS = 1280
BACK_COLS = 1280
COLS = 128
NT = (((1,), (1,)), ((), ()))
TN = (((0,), (0,)), ((), ()))
AROUND = (2, 1, -1)
VMEM_LIMIT = 40 * 1024 * 1024


def shifted(x, shift):
    n = lax.axis_size("dp")
    return lax.ppermute(x, "dp", [(i, (i + shift) % n) for i in range(n)])


def toward(x):
    n, m = lax.axis_size("dp"), lax.axis_size("ep")
    pairs = []
    for i in range(n):
        for e in range(m):
            step = 1 if e % 2 == 0 else -1
            pairs.append((i * m + e, (i + step) % n * m + e))
    return lax.ppermute(x, ("dp", "ep"), pairs)


def hbm(shape):
    return pltpu.HBM(shape, jnp.bfloat16)


def from_hbm(*arrays):
    return [pltpu.with_memory_space_constraint(x, pltpu.HBM) for x in arrays]


def dot_f32(a, b):
    return jnp.dot(a, b, preferred_element_type=jnp.float32)


def split_hi_lo(x):
    hi = x.astype(jnp.bfloat16)
    lo = (x - hi.astype(jnp.float32)).astype(jnp.bfloat16)
    return hi, lo


def slot_codes(used):
    tok = used.shape[1]
    before = lax.broadcasted_iota(jnp.int32, (tok, tok), 0) < lax.broadcasted_iota(
        jnp.int32, (tok, tok), 1
    )
    ones = jnp.where(used, 1.0, 0.0)
    rank = dot_f32(
        ones.astype(jnp.bfloat16), jnp.where(before, 1.0, 0.0).astype(jnp.bfloat16)
    )
    return jnp.where(used, rank, -1.0)


def prepare_own(count, ids, weights, tokens, extended, send, hi_out, lo_out):
    top, tok = ids.shape
    feature = tokens.shape[1]
    n_experts = hi_out.shape[0] // CAP
    expert = lax.broadcasted_iota(jnp.int32, (n_experts, tok), 0)
    gates = jnp.zeros((n_experts, tok), jnp.float32)
    for k in range(top):
        gates = gates + jnp.where(expert == ids[k : k + 1, :], weights[k : k + 1, :], 0.0)
    live = lax.broadcasted_iota(jnp.int32, (n_experts, tok), 1) < count[0]
    gates = jnp.where(live, gates, 0.0)
    hi, lo = split_hi_lo(gates)
    code = slot_codes(gates > 0)
    want = lax.broadcasted_iota(jnp.int32, (n_experts, CAP, tok), 1).astype(jnp.float32)
    hit = code[:, None, :] == want
    shape = (n_experts * CAP, tok)
    one_hot = jnp.where(hit, 1.0, 0.0).reshape(shape).astype(jnp.bfloat16)
    spread = lambda g: jnp.where(hit, g.astype(jnp.float32)[:, None, :], 0.0).reshape(shape)
    hi_out[...] = spread(hi).astype(jnp.bfloat16)
    lo_out[...] = spread(lo).astype(jnp.bfloat16)
    extended[:, :feature] = tokens[...]
    extended[:, feature:] = jnp.concatenate(
        [hi.astype(jnp.float32), lo.astype(jnp.float32)], axis=1
    ).astype(jnp.bfloat16)
    step = 128
    for c in range(0, send.shape[1], step):
        send[:, c : c + step] = dot_f32(one_hot, tokens[:, c : c + step]).astype(jnp.bfloat16)


def prepare_ring(members, e0, e1, e2, e3, send, hi_out, lo_out, rows_out):
    tok, width = e0.shape
    feature = rows_out.shape[1]
    blocks = 4
    n_experts = hi_out.shape[0] // (blocks * CAP)
    first = feature - send.shape[1]
    parts = []
    his = []
    los = []
    for j, e in enumerate((e0, e1, e2, e3)):
        rows_out[j * tok : (j + 1) * tok, :] = e[:, :feature]
        meta = e[:, feature:].astype(jnp.float32)
        hi = meta[:, :tok]
        his.append(hi)
        los.append(meta[:, tok:])
        parts.append(slot_codes(hi > 0))
    code = jnp.concatenate(parts, axis=1)
    hi = jnp.concatenate(his, axis=1)
    lo = jnp.concatenate(los, axis=1)
    rows = blocks * tok
    chunk = 16
    shape = (chunk, blocks * CAP, rows)
    slot = lax.broadcasted_iota(jnp.int32, shape, 1)
    at = lax.broadcasted_iota(jnp.int32, shape, 2)
    block = slot // CAP
    odd = lax.broadcasted_iota(jnp.int32, shape, 0) // members % 2 == 1
    block = jnp.where(odd & (block == 1), 2, jnp.where(odd & (block == 2), 1, block))
    want = jnp.where(at // tok == block, slot % CAP, -2).astype(jnp.float32)
    flat = chunk * blocks * CAP
    for c in range(0, n_experts, chunk):
        hit = code[c : c + chunk, None, :] == want
        out = slice(c * blocks * CAP, c * blocks * CAP + flat)
        one_hot = jnp.where(hit, 1.0, 0.0).reshape(flat, rows).astype(jnp.bfloat16)
        spread = lambda g: (
            jnp.where(hit, g[c : c + chunk, None, :], 0.0).reshape(flat, rows).astype(jnp.bfloat16)
        )
        hi_out[out, :] = spread(hi)
        lo_out[out, :] = spread(lo)
        send[out, :] = dot_f32(one_hot, rows_out[:, first:]).astype(jnp.bfloat16)


def call_prepare_own(count, ids, weights, tokens, n_experts, cols):
    tok, feature = tokens.shape
    slots = n_experts * CAP
    return pl.pallas_call(
        prepare_own,
        in_specs=[pl.BlockSpec(memory_space=pltpu.SMEM)] + [pl.BlockSpec()] * 3,
        out_shape=[
            jax.ShapeDtypeStruct((tok, feature + 2 * tok), jnp.bfloat16),
            hbm((slots, cols)),
            hbm((slots, tok)),
            hbm((slots, tok)),
        ],
        compiler_params=pltpu.CompilerParams(vmem_limit_bytes=24 * 1024 * 1024),
        name="prepare_own",
    )(count, *from_hbm(ids, weights, tokens))


def call_prepare_ring(around, members, n_experts, feature, cols):
    tok = around[0].shape[0]
    rows = len(around) * tok
    slots = n_experts * CAP * len(around)
    return pl.pallas_call(
        functools.partial(prepare_ring, members),
        out_shape=[
            hbm((slots, cols)),
            hbm((slots, rows)),
            hbm((slots, rows)),
            hbm((rows, feature)),
        ],
        compiler_params=pltpu.CompilerParams(vmem_limit_bytes=24 * 1024 * 1024),
        name="prepare_ring",
    )(*around)


def expert_kernel(splits, *refs):
    n_x = sum(len(s) for s in splits)
    xin, (xb, wg, wu, wd) = refs[:n_x], refs[n_x : n_x + 4]
    rest = refs[n_x + 4 :]
    rest = rest[len(rest) - (n_x + 3) :]
    outs, (ob, xs, keep) = rest[:n_x], rest[n_x:]
    member = pl.program_id(0)
    sc, bc = xin[0].shape[-1], outs[0].shape[-1]
    feature = wg.shape[2]
    n_ep, slots = xb.shape[:2]
    rows = n_ep * CAP
    planes = len(splits)
    at = 0
    place = []
    for p, split in enumerate(splits):
        row = p * rows
        for n in split:
            place.append((xin[at], outs[at], row, n))
            row += n * CAP
            at += 1
    for x, _, row, n in place:
        for c in range(0, sc, COLS):
            part = x[:, :, c : c + COLS].astype(jnp.float32).reshape(n, 2, CAP, COLS)
            part = jnp.where(member == 0, part[:, 0], part[:, 1])
            xs[row : row + n * CAP, c : c + COLS] = part.reshape(n * CAP, COLS).astype(jnp.bfloat16)
    for c in range(0, feature - sc, COLS):
        part = xb[:, :, c : c + COLS].astype(jnp.float32).reshape(n_ep, planes, CAP, COLS)
        for p in range(planes):
            xs[p * rows : (p + 1) * rows, sc + c : sc + c + COLS] = (
                part[:, p].reshape(rows, COLS).astype(jnp.bfloat16)
            )
    gate = lax.dot_general(wg[0], xs[...], NT, preferred_element_type=jnp.float32)
    up = lax.dot_general(wu[0], xs[...], NT, preferred_element_type=jnp.float32)
    hidden = (gate / (1.0 + jnp.exp(-gate)) * up).astype(jnp.bfloat16)
    out = lax.dot_general(hidden, wd[0], TN, preferred_element_type=jnp.float32)
    for c in range(0, feature - bc, COLS):
        part = out[:, bc + c : bc + c + COLS].reshape(planes, n_ep, CAP, COLS)
        part = jnp.stack([part[p] for p in range(planes)], axis=1)
        ob[:, :, c : c + COLS] = part.reshape(n_ep, slots, COLS).astype(jnp.bfloat16)

    @pl.when(member == 0)
    def _():
        keep[...] = out[:, :bc]

    @pl.when(member == 1)
    def _():
        for _, o, row, n in place:
            for c in range(0, bc, COLS):
                parts = [
                    keep[row : row + n * CAP, c : c + COLS].reshape(n, CAP, COLS),
                    out[row : row + n * CAP, c : c + COLS].reshape(n, CAP, COLS),
                ]
                o[:, :, c : c + COLS] = (
                    jnp.stack(parts, axis=1).reshape(n, 2 * CAP, COLS).astype(jnp.bfloat16)
                )


def run_experts(planes, pair, xb, sofar, wg, wu, wd, back):
    members, ffe, feature = wg.shape
    xin = [x for plane in planes for x in plane]
    splits = tuple(tuple(x.shape[0] for x in plane) for plane in planes)
    n_ep, slots, cols_b = xb.shape
    step = len(planes) * CAP
    pairs = slots // (members * step)
    rows = len(planes) * n_ep * CAP
    whole = lambda shape: pl.BlockSpec(shape, lambda m: (0,) * len(shape))
    one = lambda shape: pl.BlockSpec((1,) + shape, lambda m: (m,) + (0,) * len(shape))
    slot = lambda cols: pl.BlockSpec((n_ep, step, cols), lambda m: (0, m * pairs + pair, 0))
    out_x = [hbm(x.shape[:2] + (back,)) for x in xin]
    operands = from_hbm(*xin, xb, wg, wu, wd)
    in_specs = [whole(x.shape) for x in xin] + [slot(cols_b)] + [one((ffe, feature))] * 3
    aliases = {}
    if sofar is not None:
        aliases = {len(operands): len(xin)}
        operands.append(sofar)
        in_specs.append(pl.BlockSpec(memory_space=pl.ANY))
    return pl.pallas_call(
        functools.partial(expert_kernel, splits),
        grid=(members,),
        in_specs=in_specs,
        out_specs=[whole(x.shape) for x in out_x] + [slot(feature - back)],
        out_shape=out_x + [hbm((n_ep, slots, feature - back))],
        scratch_shapes=[
            pltpu.VMEM((rows, feature), jnp.bfloat16),
            pltpu.VMEM((rows, back), jnp.float32),
        ],
        input_output_aliases=aliases,
        compiler_params=pltpu.CompilerParams(vmem_limit_bytes=VMEM_LIMIT),
        cost_estimate=pl.CostEstimate(
            flops=members * rows * ffe * feature * 6,
            bytes_accessed=members * (rows * feature * 4 + 3 * ffe * feature * 2),
            transcendentals=members * rows * ffe,
        ),
        name="experts",
    )(*operands)


def weigh(hi, lo, values):
    return lax.dot_general(hi, values, TN, preferred_element_type=jnp.float32) + lax.dot_general(
        lo, values, TN, preferred_element_type=jnp.float32
    )


def combine(hi, lo, values, shared, *outs):
    tok, feature = outs[0].shape
    bc = feature - values.shape[1]
    for c in range(0, feature, COLS):
        cols = slice(c, c + COLS)
        total = shared[:, cols]
        if c >= bc:
            total = total + weigh(hi[...], lo[...], values[:, c - bc : c - bc + COLS])
        for j, o in enumerate(outs):
            o[:, cols] = total[j * tok : (j + 1) * tok].astype(jnp.bfloat16)


def call_combine(hi, lo, values, shared, tok):
    rows, feature = shared.shape
    return pl.pallas_call(
        combine,
        out_shape=[jax.ShapeDtypeStruct((tok, feature), jnp.bfloat16)] * (rows // tok),
        compiler_params=pltpu.CompilerParams(vmem_limit_bytes=24 * 1024 * 1024),
        name="combine",
    )(*from_hbm(hi, lo, values, shared))


def finish(hi, lo, values, total, out):
    bc = values.shape[1]
    out[:, bc:] = total[:, bc:].astype(jnp.bfloat16)
    for c in range(0, bc, COLS):
        cols = slice(c, c + COLS)
        out[:, cols] = (total[:, cols] + weigh(hi[...], lo[...], values[:, cols])).astype(
            jnp.bfloat16
        )


def call_finish(hi, lo, values, total):
    return pl.pallas_call(
        finish,
        out_shape=jax.ShapeDtypeStruct(total.shape, jnp.bfloat16),
        compiler_params=pltpu.CompilerParams(vmem_limit_bytes=16 * 1024 * 1024),
        name="finish",
    )(*from_hbm(hi, lo, values), total)


def on_device(
    tokens,
    row_counts,
    expert_ids,
    gate_weights,
    expert_gate,
    expert_up,
    expert_down,
    shared_gate,
    shared_up,
    shared_down,
):
    tok, feature = tokens.shape
    members = expert_gate.shape[0]
    n_ep = lax.axis_size("ep")
    n_dp = lax.axis_size("dp")
    n_experts = members * n_ep
    sc, bc = SEND_COLS, BACK_COLS

    def over_ep(x, rows, cols):
        return lax.all_to_all(
            x.reshape(n_ep, rows, cols), "ep", split_axis=0, concat_axis=0, tiled=True
        )

    extended, send_d, hi_d, lo_d = call_prepare_own(
        row_counts, expert_ids.T, gate_weights.T, tokens, n_experts, sc
    )
    own = over_ep(send_d, members * CAP, sc)

    around = [shifted(extended, s) for s in AROUND] + [extended]
    send_b, hi_b, lo_b, gathered = call_prepare_ring(
        around, members, n_experts, feature, feature - sc
    )

    half = n_ep // 2
    own_parts = [own[:half], own[half:]]
    behind = [toward(x) for x in own_parts]
    far = [toward(x) for x in behind]
    ahead = [toward(x) for x in far]
    came_b = over_ep(send_b, members * n_dp * CAP, feature - sc)

    gate_act = dot_f32(gathered, shared_gate)
    up_act = dot_f32(gathered, shared_up)
    hidden = (jax.nn.silu(gate_act) * up_act).astype(jnp.bfloat16)
    shared = dot_f32(hidden, shared_down)
    came_b, shared = lax.optimization_barrier((came_b, shared))

    weights = (expert_gate.swapaxes(1, 2), expert_up.swapaxes(1, 2), expert_down)
    f0, f1, b0, b1, out_b = run_experts([far, behind], 0, came_b, None, *weights, bc)
    a0, a1, o0, o1, out_b = run_experts([ahead, own_parts], 1, came_b, out_b, *weights, bc)
    ret_b = over_ep(out_b, members * n_dp * CAP, feature - bc)

    f32 = lambda x: x.astype(jnp.float32)
    ends = []
    for first, second, third, last in ((b0, f0, a0, o0), (b1, f1, a1, o1)):
        passing = first
        for mine in (second, third):
            passing = (f32(mine) + f32(toward(passing))).astype(jnp.bfloat16)
        ends.append((f32(last) + f32(toward(passing))).astype(jnp.bfloat16))
    back_d = jnp.concatenate(ends)
    back_d, ret_b = lax.optimization_barrier((back_d, ret_b))
    ret_d = over_ep(back_d, members * CAP, bc)

    *parts, kept = call_combine(hi_b, lo_b, ret_b.reshape(-1, feature - bc), shared, tok)
    live = jnp.arange(tok, dtype=jnp.int32) < row_counts[0]
    total = f32(kept)
    for part, s in zip(parts, AROUND):
        total = total + f32(shifted(part, -s))
    total = jnp.where(live[:, None], total, 0.0)
    return call_finish(hi_d, lo_d, ret_d.reshape(-1, bc), total)


def solution(mesh):
    in_specs = (
        P(("dp", "ep"), None),
        P(("dp", "ep")),
        P(("dp", "ep"), None),
        P(("dp", "ep"), None),
        P("ep", None, "dp"),
        P("ep", None, "dp"),
        P("ep", "dp", None),
        P(None, "dp"),
        P(None, "dp"),
        P("dp", None),
    )
    out_specs = P(("dp", "ep"), None)
    return jax.shard_map(
        on_device, mesh=mesh, in_specs=in_specs, out_specs=out_specs, check_vma=False
    )
```

```python
import functools

import jax
import jax.numpy as jnp
from jax import lax
from jax.experimental import pallas as pl
from jax.experimental.pallas import tpu as pltpu
from jax.sharding import PartitionSpec as P

CAP = 8
SEND_COLS = 1280
BACK_COLS = 1280
COLS = 128
NT = (((1,), (1,)), ((), ()))
TN = (((0,), (0,)), ((), ()))
AROUND = (2, 1, -1)
VMEM_LIMIT = 40 * 1024 * 1024


def shifted(x, shift):
    n = lax.axis_size("dp")
    return lax.ppermute(x, "dp", [(i, (i + shift) % n) for i in range(n)])


def toward(x):
    n, m = lax.axis_size("dp"), lax.axis_size("ep")
    pairs = []
    for i in range(n):
        for e in range(m):
            step = 1 if e % 2 == 0 else -1
            pairs.append((i * m + e, (i + step) % n * m + e))
    return lax.ppermute(x, ("dp", "ep"), pairs)


def hbm(shape):
    return pltpu.HBM(shape, jnp.bfloat16)


def from_hbm(*arrays):
    return [pltpu.with_memory_space_constraint(x, pltpu.HBM) for x in arrays]


def dot_f32(a, b):
    return jnp.dot(a, b, preferred_element_type=jnp.float32)


def split_hi_lo(x):
    hi = x.astype(jnp.bfloat16)
    lo = (x - hi.astype(jnp.float32)).astype(jnp.bfloat16)
    return hi, lo


def slot_codes(used):
    tok = used.shape[1]
    before = lax.broadcasted_iota(jnp.int32, (tok, tok), 0) < lax.broadcasted_iota(
        jnp.int32, (tok, tok), 1
    )
    ones = jnp.where(used, 1.0, 0.0)
    rank = dot_f32(
        ones.astype(jnp.bfloat16), jnp.where(before, 1.0, 0.0).astype(jnp.bfloat16)
    )
    return jnp.where(used, rank, -1.0)


def prepare_own(count, ids, weights, tokens, extended, send, hi_out, lo_out):
    top, tok = ids.shape
    feature = tokens.shape[1]
    n_experts = hi_out.shape[0] // CAP
    expert = lax.broadcasted_iota(jnp.int32, (n_experts, tok), 0)
    gates = jnp.zeros((n_experts, tok), jnp.float32)
    for k in range(top):
        gates = gates + jnp.where(expert == ids[k : k + 1, :], weights[k : k + 1, :], 0.0)
    live = lax.broadcasted_iota(jnp.int32, (n_experts, tok), 1) < count[0]
    gates = jnp.where(live, gates, 0.0)
    hi, lo = split_hi_lo(gates)
    code = slot_codes(gates > 0)
    want = lax.broadcasted_iota(jnp.int32, (n_experts, CAP, tok), 1).astype(jnp.float32)
    hit = code[:, None, :] == want
    shape = (n_experts * CAP, tok)
    one_hot = jnp.where(hit, 1.0, 0.0).reshape(shape).astype(jnp.bfloat16)
    spread = lambda g: jnp.where(hit, g.astype(jnp.float32)[:, None, :], 0.0).reshape(shape)
    hi_out[...] = spread(hi).astype(jnp.bfloat16)
    lo_out[...] = spread(lo).astype(jnp.bfloat16)
    extended[:, :feature] = tokens[...]
    extended[:, feature:] = jnp.concatenate(
        [hi.astype(jnp.float32), lo.astype(jnp.float32)], axis=1
    ).astype(jnp.bfloat16)
    step = 128
    for c in range(0, send.shape[1], step):
        send[:, c : c + step] = dot_f32(one_hot, tokens[:, c : c + step]).astype(jnp.bfloat16)


def prepare_ring(members, e0, e1, e2, e3, send, hi_out, lo_out, rows_out):
    tok, width = e0.shape
    feature = rows_out.shape[1]
    blocks = 4
    n_experts = hi_out.shape[0] // (blocks * CAP)
    first = feature - send.shape[1]
    parts = []
    his = []
    los = []
    for j, e in enumerate((e0, e1, e2, e3)):
        rows_out[j * tok : (j + 1) * tok, :] = e[:, :feature]
        meta = e[:, feature:].astype(jnp.float32)
        hi = meta[:, :tok]
        his.append(hi)
        los.append(meta[:, tok:])
        parts.append(slot_codes(hi > 0))
    code = jnp.concatenate(parts, axis=1)
    hi = jnp.concatenate(his, axis=1)
    lo = jnp.concatenate(los, axis=1)
    rows = blocks * tok
    chunk = 16
    shape = (chunk, blocks * CAP, rows)
    slot = lax.broadcasted_iota(jnp.int32, shape, 1)
    at = lax.broadcasted_iota(jnp.int32, shape, 2)
    block = slot // CAP
    odd = lax.broadcasted_iota(jnp.int32, shape, 0) // members % 2 == 1
    block = jnp.where(odd & (block == 1), 2, jnp.where(odd & (block == 2), 1, block))
    want = jnp.where(at // tok == block, slot % CAP, -2).astype(jnp.float32)
    flat = chunk * blocks * CAP
    for c in range(0, n_experts, chunk):
        hit = code[c : c + chunk, None, :] == want
        out = slice(c * blocks * CAP, c * blocks * CAP + flat)
        one_hot = jnp.where(hit, 1.0, 0.0).reshape(flat, rows).astype(jnp.bfloat16)
        spread = lambda g: (
            jnp.where(hit, g[c : c + chunk, None, :], 0.0).reshape(flat, rows).astype(jnp.bfloat16)
        )
        hi_out[out, :] = spread(hi)
        lo_out[out, :] = spread(lo)
        send[out, :] = dot_f32(one_hot, rows_out[:, first:]).astype(jnp.bfloat16)


def call_prepare_own(count, ids, weights, tokens, n_experts, cols):
    tok, feature = tokens.shape
    slots = n_experts * CAP
    return pl.pallas_call(
        prepare_own,
        in_specs=[pl.BlockSpec(memory_space=pltpu.SMEM)] + [pl.BlockSpec()] * 3,
        out_shape=[
            jax.ShapeDtypeStruct((tok, feature + 2 * tok), jnp.bfloat16),
            hbm((slots, cols)),
            hbm((slots, tok)),
            hbm((slots, tok)),
        ],
        compiler_params=pltpu.CompilerParams(vmem_limit_bytes=24 * 1024 * 1024),
        name="prepare_own",
    )(count, *from_hbm(ids, weights, tokens))


def call_prepare_ring(around, members, n_experts, feature, cols):
    tok = around[0].shape[0]
    rows = len(around) * tok
    slots = n_experts * CAP * len(around)
    return pl.pallas_call(
        functools.partial(prepare_ring, members),
        out_shape=[
            hbm((slots, cols)),
            hbm((slots, rows)),
            hbm((slots, rows)),
            hbm((rows, feature)),
        ],
        compiler_params=pltpu.CompilerParams(vmem_limit_bytes=24 * 1024 * 1024),
        name="prepare_ring",
    )(*around)


def expert_kernel(planes, pair, *refs):
    n_x = planes * 2
    xin, (xb, wg, wu, wd) = refs[:n_x], refs[n_x : n_x + 4]
    rest = refs[len(refs) - (n_x + 10) :]
    outs, ob = rest[:n_x], rest[n_x]
    xbb, obb, obuf, wgb, wub, wdb, xs, in_sems, out_sems = rest[n_x + 1 :]
    members = wg.shape[0]
    rows, sc = xin[0].shape
    bc = outs[0].shape[-1]
    feature = wg.shape[2]
    n_ep = xb.shape[0]
    slots = planes * CAP
    pairs = xb.shape[1] // (members * slots)
    fetched, sent = [], []

    def fetch(src, dst):
        copy = pltpu.make_async_copy(src, dst, in_sems.at[len(fetched)])
        copy.start()
        fetched.append(copy)
        return copy

    def send(src, dst):
        copy = pltpu.make_async_copy(src, dst, out_sems.at[len(sent)])
        copy.start()
        sent.append(copy)

    chunk = lambda m: pl.ds((m * pairs + pair) * slots, slots)
    got = []
    for m in range(members):
        copies = [
            fetch(xin[p * members + m], xs.at[m, pl.ds(p * rows, rows), pl.ds(0, sc)])
            for p in range(planes)
        ]
        copies.append(fetch(xb.at[:, chunk(m)], xbb.at[m]))
        copies += [fetch(w.at[m], buf.at[m]) for w, buf in ((wg, wgb), (wu, wub), (wd, wdb))]
        got.append(copies)
    for m in range(members):
        for copy in got[m][: planes + 1]:
            copy.wait()
        for c in range(0, feature - sc, COLS):
            part = xbb[m, :, :, c : c + COLS].astype(jnp.float32).reshape(n_ep, planes, CAP, COLS)
            for p in range(planes):
                xs[m, p * rows : (p + 1) * rows, sc + c : sc + c + COLS] = (
                    part[:, p].reshape(rows, COLS).astype(jnp.bfloat16)
                )
        got[m][planes + 1].wait()
        gate = lax.dot_general(wgb[m], xs[m], NT, preferred_element_type=jnp.float32)
        got[m][planes + 2].wait()
        up = lax.dot_general(wub[m], xs[m], NT, preferred_element_type=jnp.float32)
        hidden = (gate / (1.0 + jnp.exp(-gate)) * up).astype(jnp.bfloat16)
        got[m][planes + 3].wait()
        out = lax.dot_general(hidden, wdb[m], TN, preferred_element_type=jnp.float32)
        for p in range(planes):
            obuf[m, p] = out[p * rows : (p + 1) * rows, :bc].astype(jnp.bfloat16)
            send(obuf.at[m, p], outs[p * members + m])
        for c in range(0, feature - bc, COLS):
            part = out[:, bc + c : bc + c + COLS].reshape(planes, n_ep, CAP, COLS)
            part = jnp.stack([part[p] for p in range(planes)], axis=1)
            obb[m, :, :, c : c + COLS] = part.reshape(n_ep, slots, COLS).astype(jnp.bfloat16)
        send(obb.at[m], ob.at[:, chunk(m)])
    for copy in sent:
        copy.wait()


def run_experts(planes, pair, xb, sofar, wg, wu, wd, back):
    members, ffe, feature = wg.shape
    xin = [x for plane in planes for x in plane]
    n_ep, slots, cols_b = xb.shape
    step = len(planes) * CAP
    rows = len(planes) * n_ep * CAP
    bf = jnp.bfloat16
    out_x = [hbm((x.shape[0], back)) for x in xin]
    operands = from_hbm(*xin, xb, wg, wu, wd)
    aliases = {}
    if sofar is not None:
        aliases = {len(operands): len(xin)}
        operands.append(sofar)
    return pl.pallas_call(
        functools.partial(expert_kernel, len(planes), pair),
        in_specs=[pl.BlockSpec(memory_space=pltpu.HBM)] * len(operands),
        out_specs=[pl.BlockSpec(memory_space=pltpu.HBM)] * (len(out_x) + 1),
        out_shape=out_x + [hbm((n_ep, slots, feature - back))],
        scratch_shapes=[
            pltpu.VMEM((members, n_ep, step, cols_b), bf),
            pltpu.VMEM((members, n_ep, step, feature - back), bf),
            pltpu.VMEM((members, len(planes), n_ep * CAP, back), bf),
            pltpu.VMEM((members, ffe, feature), bf),
            pltpu.VMEM((members, ffe, feature), bf),
            pltpu.VMEM((members, ffe, feature), bf),
            pltpu.VMEM((members, rows, feature), bf),
            pltpu.SemaphoreType.DMA((members * (len(planes) + 4),)),
            pltpu.SemaphoreType.DMA((members * (len(planes) + 1),)),
        ],
        input_output_aliases=aliases,
        compiler_params=pltpu.CompilerParams(vmem_limit_bytes=VMEM_LIMIT),
        cost_estimate=pl.CostEstimate(
            flops=members * rows * ffe * feature * 6,
            bytes_accessed=members * (rows * feature * 4 + 3 * ffe * feature * 2),
            transcendentals=members * rows * ffe,
        ),
        name="experts",
    )(*operands)


def weigh(hi, lo, values):
    return dot_f32(hi, values) + dot_f32(lo, values)


def combine(hi, lo, values, shared, *outs):
    tok, feature = outs[0].shape
    bc = feature - values.shape[1]
    late = shared[:, bc:] + weigh(hi[...], lo[...], values[...])
    for j, o in enumerate(outs):
        rows = slice(j * tok, (j + 1) * tok)
        o[:, :bc] = shared[rows, :bc].astype(jnp.bfloat16)
        o[:, bc:] = late[rows].astype(jnp.bfloat16)


def call_combine(hi, lo, values, shared, tok):
    rows, feature = shared.shape
    return pl.pallas_call(
        combine,
        out_shape=[jax.ShapeDtypeStruct((tok, feature), jnp.bfloat16)] * (rows // tok),
        compiler_params=pltpu.CompilerParams(vmem_limit_bytes=24 * 1024 * 1024),
        name="combine",
    )(*from_hbm(hi, lo, values, shared))


def finish(hi, lo, values, total, out):
    bc = values.shape[1]
    out[:, bc:] = total[:, bc:].astype(jnp.bfloat16)
    out[:, :bc] = (total[:, :bc] + weigh(hi[...], lo[...], values[...])).astype(jnp.bfloat16)


def call_finish(hi, lo, values, total):
    return pl.pallas_call(
        finish,
        out_shape=jax.ShapeDtypeStruct(total.shape, jnp.bfloat16),
        compiler_params=pltpu.CompilerParams(vmem_limit_bytes=16 * 1024 * 1024),
        name="finish",
    )(*from_hbm(hi, lo, values), total)


def on_device(
    tokens,
    row_counts,
    expert_ids,
    gate_weights,
    expert_gate,
    expert_up,
    expert_down,
    shared_gate,
    shared_up,
    shared_down,
):
    tok, feature = tokens.shape
    members = expert_gate.shape[0]
    n_ep = lax.axis_size("ep")
    n_dp = lax.axis_size("dp")
    n_experts = members * n_ep
    sc, bc = SEND_COLS, BACK_COLS

    def over_ep(x, rows, cols):
        return lax.all_to_all(
            x.reshape(n_ep, rows, cols), "ep", split_axis=0, concat_axis=0, tiled=True
        )

    extended, send_d, hi_d, lo_d = call_prepare_own(
        row_counts, expert_ids.T, gate_weights.T, tokens, n_experts, sc
    )
    own = over_ep(send_d, members * CAP, sc)

    around = [shifted(extended, s) for s in AROUND] + [extended]
    send_b, hi_b, lo_b, gathered = call_prepare_ring(
        around, members, n_experts, feature, feature - sc
    )

    weights = (expert_gate.swapaxes(1, 2), expert_up.swapaxes(1, 2), expert_down)

    own_slots = own.reshape(n_ep, members, CAP, sc)
    own_parts = [own_slots[:, m].reshape(n_ep * CAP, sc) for m in range(members)]
    behind = [toward(x) for x in own_parts]
    far = [toward(x) for x in behind]
    ahead = [toward(x) for x in far]
    came_b = over_ep(send_b, members * n_dp * CAP, feature - sc)

    gate_act = dot_f32(gathered, shared_gate)
    up_act = dot_f32(gathered, shared_up)
    hidden = (jax.nn.silu(gate_act) * up_act).astype(jnp.bfloat16)
    shared = dot_f32(hidden, shared_down)
    hi_b, lo_b, hi_d, lo_d = hi_b.T, lo_b.T, hi_d.T, lo_d.T
    came_b, shared, hi_b, lo_b, hi_d, lo_d = lax.optimization_barrier(
        (came_b, shared, hi_b, lo_b, hi_d, lo_d)
    )

    f0, f1, b0, b1, out_b = run_experts([far, behind], 0, came_b, None, *weights, bc)
    a0, a1, o0, o1, out_b = run_experts([ahead, own_parts], 1, came_b, out_b, *weights, bc)
    ret_b = over_ep(out_b, members * n_dp * CAP, feature - bc)

    f32 = lambda x: x.astype(jnp.float32)
    ends = []
    for first, second, third, last in ((b0, f0, a0, o0), (b1, f1, a1, o1)):
        passing = first
        for mine in (second, third):
            passing = (f32(mine) + f32(toward(passing))).astype(jnp.bfloat16)
        ends.append((f32(last) + f32(toward(passing))).astype(jnp.bfloat16))
    back_d = jnp.stack([x.reshape(n_ep, CAP, bc) for x in ends], axis=1)
    back_d, ret_b = lax.optimization_barrier((back_d, ret_b))
    ret_d = over_ep(back_d, members * CAP, bc)

    *parts, kept = call_combine(hi_b, lo_b, ret_b.reshape(-1, feature - bc), shared, tok)
    live = jnp.arange(tok, dtype=jnp.int32) < row_counts[0]
    total = f32(kept)
    for part, s in zip(parts, AROUND):
        total = total + f32(shifted(part, -s))
    total = jnp.where(live[:, None], total, 0.0)
    return call_finish(hi_d, lo_d, ret_d.reshape(-1, bc), total)


def solution(mesh):
    in_specs = (
        P(("dp", "ep"), None),
        P(("dp", "ep")),
        P(("dp", "ep"), None),
        P(("dp", "ep"), None),
        P("ep", None, "dp"),
        P("ep", None, "dp"),
        P("ep", "dp", None),
        P(None, "dp"),
        P(None, "dp"),
        P("dp", None),
    )
    out_specs = P(("dp", "ep"), None)
    return jax.shard_map(
        on_device, mesh=mesh, in_specs=in_specs, out_specs=out_specs, check_vma=False
    )
```

```python
import functools

import jax
import jax.numpy as jnp
from jax import lax
from jax.experimental import pallas as pl
from jax.experimental.pallas import tpu as pltpu
from jax.sharding import PartitionSpec as P

CAP = 8
SEND_COLS = 1280
BACK_COLS = 1280
COLS = 128
NT = (((1,), (1,)), ((), ()))
TN = (((0,), (0,)), ((), ()))
AROUND = (2, 1, -1)
VMEM_LIMIT = 40 * 1024 * 1024


def shifted(x, shift):
    n = lax.axis_size("dp")
    return lax.ppermute(x, "dp", [(i, (i + shift) % n) for i in range(n)])


def toward(x):
    n, m = lax.axis_size("dp"), lax.axis_size("ep")
    pairs = []
    for i in range(n):
        for e in range(m):
            step = 1 if e % 2 == 0 else -1
            pairs.append((i * m + e, (i + step) % n * m + e))
    return lax.ppermute(x, ("dp", "ep"), pairs)


def hbm(shape):
    return pltpu.HBM(shape, jnp.bfloat16)


def from_hbm(*arrays):
    return [pltpu.with_memory_space_constraint(x, pltpu.HBM) for x in arrays]


def dot_f32(a, b):
    return jnp.dot(a, b, preferred_element_type=jnp.float32)


def split_hi_lo(x):
    hi = x.astype(jnp.bfloat16)
    lo = (x - hi.astype(jnp.float32)).astype(jnp.bfloat16)
    return hi, lo


def slot_codes(used):
    tok = used.shape[1]
    before = lax.broadcasted_iota(jnp.int32, (tok, tok), 0) < lax.broadcasted_iota(
        jnp.int32, (tok, tok), 1
    )
    ones = jnp.where(used, 1.0, 0.0)
    rank = dot_f32(
        ones.astype(jnp.bfloat16), jnp.where(before, 1.0, 0.0).astype(jnp.bfloat16)
    )
    return jnp.where(used, rank, -1.0)


def prepare_own(count, ids, weights, tokens, extended, send, hi_out, lo_out):
    top, tok = ids.shape
    feature = tokens.shape[1]
    n_experts = hi_out.shape[0] // CAP
    expert = lax.broadcasted_iota(jnp.int32, (n_experts, tok), 0)
    gates = jnp.zeros((n_experts, tok), jnp.float32)
    for k in range(top):
        gates = gates + jnp.where(expert == ids[k : k + 1, :], weights[k : k + 1, :], 0.0)
    live = lax.broadcasted_iota(jnp.int32, (n_experts, tok), 1) < count[0]
    gates = jnp.where(live, gates, 0.0)
    hi, lo = split_hi_lo(gates)
    code = slot_codes(gates > 0)
    want = lax.broadcasted_iota(jnp.int32, (n_experts, CAP, tok), 1).astype(jnp.float32)
    hit = code[:, None, :] == want
    shape = (n_experts * CAP, tok)
    one_hot = jnp.where(hit, 1.0, 0.0).reshape(shape).astype(jnp.bfloat16)
    spread = lambda g: jnp.where(hit, g.astype(jnp.float32)[:, None, :], 0.0).reshape(shape)
    hi_out[...] = spread(hi).astype(jnp.bfloat16)
    lo_out[...] = spread(lo).astype(jnp.bfloat16)
    extended[:, :feature] = tokens[...]
    extended[:, feature:] = jnp.concatenate(
        [hi.astype(jnp.float32), lo.astype(jnp.float32)], axis=1
    ).astype(jnp.bfloat16)
    step = 128
    for c in range(0, send.shape[1], step):
        send[:, c : c + step] = dot_f32(one_hot, tokens[:, c : c + step]).astype(jnp.bfloat16)


def prepare_ring(members, e0, e1, e2, e3, send, hi_out, lo_out, rows_out):
    tok, width = e0.shape
    feature = rows_out.shape[1]
    blocks = 4
    n_experts = hi_out.shape[0] // (blocks * CAP)
    first = feature - send.shape[1]
    parts = []
    his = []
    los = []
    for j, e in enumerate((e0, e1, e2, e3)):
        rows_out[j * tok : (j + 1) * tok, :] = e[:, :feature]
        meta = e[:, feature:].astype(jnp.float32)
        hi = meta[:, :tok]
        his.append(hi)
        los.append(meta[:, tok:])
        parts.append(slot_codes(hi > 0))
    code = jnp.concatenate(parts, axis=1)
    hi = jnp.concatenate(his, axis=1)
    lo = jnp.concatenate(los, axis=1)
    rows = blocks * tok
    chunk = 16
    shape = (chunk, blocks * CAP, rows)
    slot = lax.broadcasted_iota(jnp.int32, shape, 1)
    at = lax.broadcasted_iota(jnp.int32, shape, 2)
    block = slot // CAP
    odd = lax.broadcasted_iota(jnp.int32, shape, 0) // members % 2 == 1
    block = jnp.where(odd & (block == 1), 2, jnp.where(odd & (block == 2), 1, block))
    want = jnp.where(at // tok == block, slot % CAP, -2).astype(jnp.float32)
    flat = chunk * blocks * CAP
    for c in range(0, n_experts, chunk):
        hit = code[c : c + chunk, None, :] == want
        out = slice(c * blocks * CAP, c * blocks * CAP + flat)
        one_hot = jnp.where(hit, 1.0, 0.0).reshape(flat, rows).astype(jnp.bfloat16)
        spread = lambda g: (
            jnp.where(hit, g[c : c + chunk, None, :], 0.0).reshape(flat, rows).astype(jnp.bfloat16)
        )
        hi_out[out, :] = spread(hi)
        lo_out[out, :] = spread(lo)
        send[out, :] = dot_f32(one_hot, rows_out[:, first:]).astype(jnp.bfloat16)


def call_prepare_own(count, ids, weights, tokens, n_experts, cols):
    tok, feature = tokens.shape
    slots = n_experts * CAP
    return pl.pallas_call(
        prepare_own,
        in_specs=[pl.BlockSpec(memory_space=pltpu.SMEM)] + [pl.BlockSpec()] * 3,
        out_shape=[
            jax.ShapeDtypeStruct((tok, feature + 2 * tok), jnp.bfloat16),
            hbm((slots, cols)),
            hbm((slots, tok)),
            hbm((slots, tok)),
        ],
        compiler_params=pltpu.CompilerParams(vmem_limit_bytes=24 * 1024 * 1024),
        name="prepare_own",
    )(count, *from_hbm(ids, weights, tokens))


def call_prepare_ring(around, members, n_experts, feature, cols):
    tok = around[0].shape[0]
    rows = len(around) * tok
    slots = n_experts * CAP * len(around)
    return pl.pallas_call(
        functools.partial(prepare_ring, members),
        out_shape=[
            hbm((slots, cols)),
            hbm((slots, rows)),
            hbm((slots, rows)),
            hbm((rows, feature)),
        ],
        compiler_params=pltpu.CompilerParams(vmem_limit_bytes=24 * 1024 * 1024),
        name="prepare_ring",
    )(*around)


def expert_kernel(planes, pair, *refs):
    n_x = planes * 2
    xin, (xb, wg, wu, wd) = refs[:n_x], refs[n_x : n_x + 4]
    members = wg.shape[0]
    n_out = members + 1
    rest = refs[len(refs) - (n_out + 10) :]
    outs, ob = rest[:n_out], rest[n_out]
    xbb, obb, obuf, wgb, wub, wdb, xs, in_sems, out_sems = rest[n_out + 1 :]
    rows, sc = xin[0].shape
    bc = outs[0].shape[-1]
    feature = wg.shape[2]
    n_ep = xb.shape[0]
    slots = planes * CAP
    pairs = xb.shape[1] // (members * slots)
    fetched, sent = [], []

    def fetch(src, dst):
        copy = pltpu.make_async_copy(src, dst, in_sems.at[len(fetched)])
        copy.start()
        fetched.append(copy)
        return copy

    def send(src, dst):
        copy = pltpu.make_async_copy(src, dst, out_sems.at[len(sent)])
        copy.start()
        sent.append(copy)

    chunk = lambda m: pl.ds((m * pairs + pair) * slots, slots)
    got = []
    for m in range(members):
        copies = [
            fetch(xin[p * members + m], xs.at[m, pl.ds(p * rows, rows), pl.ds(0, sc)])
            for p in range(planes)
        ]
        copies.append(fetch(xb.at[:, chunk(m)], xbb.at[m]))
        copies += [fetch(w.at[m], buf.at[m]) for w, buf in ((wg, wgb), (wu, wub), (wd, wdb))]
        got.append(copies)
    for m in range(members):
        for copy in got[m][: planes + 1]:
            copy.wait()
        for c in range(0, feature - sc, COLS):
            part = xbb[m, :, :, c : c + COLS].astype(jnp.float32).reshape(n_ep, planes, CAP, COLS)
            for p in range(planes):
                xs[m, p * rows : (p + 1) * rows, sc + c : sc + c + COLS] = (
                    part[:, p].reshape(rows, COLS).astype(jnp.bfloat16)
                )
        got[m][planes + 1].wait()
        gate = lax.dot_general(wgb[m], xs[m], NT, preferred_element_type=jnp.float32)
        got[m][planes + 2].wait()
        up = lax.dot_general(wub[m], xs[m], NT, preferred_element_type=jnp.float32)
        hidden = (gate / (1.0 + jnp.exp(-gate)) * up).astype(jnp.bfloat16)
        got[m][planes + 3].wait()
        out = lax.dot_general(hidden, wdb[m], TN, preferred_element_type=jnp.float32)
        for p in range(planes):
            obuf[m, p] = out[p * rows : (p + 1) * rows, :bc].astype(jnp.bfloat16)
            send(obuf.at[m, p], outs[m] if p == 0 else outs[-1].at[pl.ds(m * rows, rows)])
        for c in range(0, feature - bc, COLS):
            part = out[:, bc + c : bc + c + COLS].reshape(planes, n_ep, CAP, COLS)
            part = jnp.stack([part[p] for p in range(planes)], axis=1)
            obb[m, :, :, c : c + COLS] = part.reshape(n_ep, slots, COLS).astype(jnp.bfloat16)
        send(obb.at[m], ob.at[:, chunk(m)])
    for copy in sent:
        copy.wait()


def run_experts(planes, pair, xb, sofar, wg, wu, wd, back):
    members, ffe, feature = wg.shape
    xin = [x for plane in planes for x in plane]
    n_ep, slots, cols_b = xb.shape
    step = len(planes) * CAP
    rows = len(planes) * n_ep * CAP
    bf = jnp.bfloat16
    out_x = [hbm((n_ep * CAP, back))] * members + [hbm((members * n_ep * CAP, back))]
    operands = from_hbm(*xin, xb, wg, wu, wd)
    aliases = {}
    if sofar is not None:
        aliases = {len(operands): len(out_x)}
        operands.append(sofar)
    return pl.pallas_call(
        functools.partial(expert_kernel, len(planes), pair),
        in_specs=[pl.BlockSpec(memory_space=pltpu.HBM)] * len(operands),
        out_specs=[pl.BlockSpec(memory_space=pltpu.HBM)] * (len(out_x) + 1),
        out_shape=out_x + [hbm((n_ep, slots, feature - back))],
        scratch_shapes=[
            pltpu.VMEM((members, n_ep, step, cols_b), bf),
            pltpu.VMEM((members, n_ep, step, feature - back), bf),
            pltpu.VMEM((members, len(planes), n_ep * CAP, back), bf),
            pltpu.VMEM((members, ffe, feature), bf),
            pltpu.VMEM((members, ffe, feature), bf),
            pltpu.VMEM((members, ffe, feature), bf),
            pltpu.VMEM((members, rows, feature), bf),
            pltpu.SemaphoreType.DMA((members * (len(planes) + 4),)),
            pltpu.SemaphoreType.DMA((members * (len(planes) + 1),)),
        ],
        input_output_aliases=aliases,
        compiler_params=pltpu.CompilerParams(vmem_limit_bytes=VMEM_LIMIT),
        cost_estimate=pl.CostEstimate(
            flops=20 * 10**9, bytes_accessed=20 * 10**7, transcendentals=0
        ),
        name="experts",
    )(*operands)


def last_sum(own, *refs):
    ends, out = refs[:-1], refs[-1]
    n_ep, slots, cols = out.shape
    rows = n_ep * CAP
    for c in range(0, cols, COLS):
        parts = []
        for m, end in enumerate(ends):
            mine = own[m * rows : (m + 1) * rows, c : c + COLS].astype(jnp.float32)
            came = end[:, c : c + COLS].astype(jnp.float32)
            parts.append((mine + came).reshape(n_ep, CAP, COLS))
        out[:, :, c : c + COLS] = (
            jnp.stack(parts, axis=1).reshape(n_ep, slots, COLS).astype(jnp.bfloat16)
        )


def call_last_sum(own, ends, n_ep):
    return pl.pallas_call(
        last_sum,
        out_shape=hbm((n_ep, len(ends) * CAP, own.shape[1])),
        compiler_params=pltpu.CompilerParams(vmem_limit_bytes=16 * 1024 * 1024),
        name="last_sum",
    )(*from_hbm(own, *ends))


def weigh(hi, lo, values):
    return dot_f32(hi, values) + dot_f32(lo, values)


def combine(hi, lo, values, shared, *outs):
    tok, feature = outs[0].shape
    bc = feature - values.shape[1]
    late = shared[:, bc:] + weigh(hi[...], lo[...], values[...])
    for j, o in enumerate(outs):
        rows = slice(j * tok, (j + 1) * tok)
        o[:, :bc] = shared[rows, :bc].astype(jnp.bfloat16)
        o[:, bc:] = late[rows].astype(jnp.bfloat16)


def call_combine(hi, lo, values, shared, tok):
    rows, feature = shared.shape
    return pl.pallas_call(
        combine,
        out_shape=[jax.ShapeDtypeStruct((tok, feature), jnp.bfloat16)] * (rows // tok),
        compiler_params=pltpu.CompilerParams(vmem_limit_bytes=24 * 1024 * 1024),
        name="combine",
    )(*from_hbm(hi, lo, values, shared))


def finish(hi, lo, values, total, out):
    bc = values.shape[1]
    out[:, bc:] = total[:, bc:].astype(jnp.bfloat16)
    out[:, :bc] = (total[:, :bc] + weigh(hi[...], lo[...], values[...])).astype(jnp.bfloat16)


def call_finish(hi, lo, values, total):
    return pl.pallas_call(
        finish,
        out_shape=jax.ShapeDtypeStruct(total.shape, jnp.bfloat16),
        compiler_params=pltpu.CompilerParams(vmem_limit_bytes=16 * 1024 * 1024),
        name="finish",
    )(*from_hbm(hi, lo, values), total)


def on_device(
    tokens,
    row_counts,
    expert_ids,
    gate_weights,
    expert_gate,
    expert_up,
    expert_down,
    shared_gate,
    shared_up,
    shared_down,
):
    tok, feature = tokens.shape
    members = expert_gate.shape[0]
    n_ep = lax.axis_size("ep")
    n_dp = lax.axis_size("dp")
    n_experts = members * n_ep
    sc, bc = SEND_COLS, BACK_COLS

    def over_ep(x, rows, cols):
        return lax.all_to_all(
            x.reshape(n_ep, rows, cols), "ep", split_axis=0, concat_axis=0, tiled=True
        )

    extended, send_d, hi_d, lo_d = call_prepare_own(
        row_counts, expert_ids.T, gate_weights.T, tokens, n_experts, sc
    )
    own = over_ep(send_d, members * CAP, sc)

    around = [shifted(extended, s) for s in AROUND] + [extended]
    send_b, hi_b, lo_b, gathered = call_prepare_ring(
        around, members, n_experts, feature, feature - sc
    )

    weights = (expert_gate.swapaxes(1, 2), expert_up.swapaxes(1, 2), expert_down)

    own_slots = own.reshape(n_ep, members, CAP, sc)
    own_parts = [own_slots[:, m].reshape(n_ep * CAP, sc) for m in range(members)]
    behind = [toward(x) for x in own_parts]
    far = [toward(x) for x in behind]
    ahead = [toward(x) for x in far]
    came_b = over_ep(send_b, members * n_dp * CAP, feature - sc)

    *to_far, to_behind, out_b = run_experts([far, behind], 0, came_b, None, *weights, bc)
    *to_ahead, to_own, out_b = run_experts([ahead, own_parts], 1, came_b, out_b, *weights, bc)
    out_b, gathered, hi_b, lo_b = lax.optimization_barrier((out_b, gathered, hi_b, lo_b))
    ret_b = over_ep(out_b, members * n_dp * CAP, feature - bc)

    gate_act = dot_f32(gathered, shared_gate)
    up_act = dot_f32(gathered, shared_up)
    hidden = (jax.nn.silu(gate_act) * up_act).astype(jnp.bfloat16)
    shared = dot_f32(hidden, shared_down)

    f32 = lambda x: x.astype(jnp.float32)
    rows = n_ep * CAP
    arrived = toward(to_behind)
    ends = []
    for m in range(members):
        part = slice(m * rows, (m + 1) * rows)
        passing = (f32(to_far[m]) + f32(arrived[part])).astype(jnp.bfloat16)
        passing = (f32(to_ahead[m]) + f32(toward(passing))).astype(jnp.bfloat16)
        ends.append(toward(passing))
    *ends, shared, hi_b, lo_b = lax.optimization_barrier((*ends, shared, hi_b.T, lo_b.T))
    back_d = call_last_sum(to_own, ends, n_ep)
    back_d, ret_b = lax.optimization_barrier((back_d, ret_b))
    ret_d = over_ep(back_d, members * CAP, bc)

    *parts, kept = call_combine(hi_b, lo_b, ret_b.reshape(-1, feature - bc), shared, tok)
    live = jnp.arange(tok, dtype=jnp.int32) < row_counts[0]
    total = f32(kept)
    for part, s in zip(parts, AROUND):
        total = total + f32(shifted(part, -s))
    total = jnp.where(live[:, None], total, 0.0)
    return call_finish(hi_d.T, lo_d.T, ret_d.reshape(-1, bc), total)


def solution(mesh):
    in_specs = (
        P(("dp", "ep"), None),
        P(("dp", "ep")),
        P(("dp", "ep"), None),
        P(("dp", "ep"), None),
        P("ep", None, "dp"),
        P("ep", None, "dp"),
        P("ep", "dp", None),
        P(None, "dp"),
        P(None, "dp"),
        P("dp", None),
    )
    out_specs = P(("dp", "ep"), None)
    return jax.shard_map(
        on_device, mesh=mesh, in_specs=in_specs, out_specs=out_specs, check_vma=False
    )
```

```python
import functools

import jax
import jax.numpy as jnp
from jax import lax
from jax.experimental import pallas as pl
from jax.experimental.pallas import tpu as pltpu
from jax.sharding import PartitionSpec as P

CAP = 8
SEND_COLS = 1280
BACK_COLS = 1280
COLS = 128
WIDE = 256
NT = (((1,), (1,)), ((), ()))
TN = (((0,), (0,)), ((), ()))
AROUND = (2, 1, -1)
VMEM_LIMIT = 40 * 1024 * 1024


def shifted(x, shift):
    n = lax.axis_size("dp")
    return lax.ppermute(x, "dp", [(i, (i + shift) % n) for i in range(n)])


def toward(x):
    n, m = lax.axis_size("dp"), lax.axis_size("ep")
    pairs = []
    for i in range(n):
        for e in range(m):
            step = 1 if e % 2 == 0 else -1
            pairs.append((i * m + e, (i + step) % n * m + e))
    return lax.ppermute(x, ("dp", "ep"), pairs)


def hbm(shape):
    return pltpu.HBM(shape, jnp.bfloat16)


def from_hbm(*arrays):
    return [pltpu.with_memory_space_constraint(x, pltpu.HBM) for x in arrays]


def dot_f32(a, b):
    return jnp.dot(a, b, preferred_element_type=jnp.float32)


def split_hi_lo(x):
    hi = x.astype(jnp.bfloat16)
    lo = (x - hi.astype(jnp.float32)).astype(jnp.bfloat16)
    return hi, lo


def slot_codes(used):
    tok = used.shape[1]
    before = lax.broadcasted_iota(jnp.int32, (tok, tok), 0) < lax.broadcasted_iota(
        jnp.int32, (tok, tok), 1
    )
    ones = jnp.where(used, 1.0, 0.0)
    rank = dot_f32(
        ones.astype(jnp.bfloat16), jnp.where(before, 1.0, 0.0).astype(jnp.bfloat16)
    )
    return jnp.where(used, rank, -1.0)


def prepare_own(count, ids, weights, tokens, extended, send, hi_out, lo_out):
    top, tok = ids.shape
    feature = tokens.shape[1]
    n_experts = hi_out.shape[0] // CAP
    expert = lax.broadcasted_iota(jnp.int32, (n_experts, tok), 0)
    gates = jnp.zeros((n_experts, tok), jnp.float32)
    for k in range(top):
        gates = gates + jnp.where(expert == ids[k : k + 1, :], weights[k : k + 1, :], 0.0)
    live = lax.broadcasted_iota(jnp.int32, (n_experts, tok), 1) < count[0]
    gates = jnp.where(live, gates, 0.0)
    hi, lo = split_hi_lo(gates)
    code = slot_codes(gates > 0)
    want = lax.broadcasted_iota(jnp.int32, (n_experts, CAP, tok), 1).astype(jnp.float32)
    hit = code[:, None, :] == want
    shape = (n_experts * CAP, tok)
    one_hot = jnp.where(hit, 1.0, 0.0).reshape(shape).astype(jnp.bfloat16)
    spread = lambda g: jnp.where(hit, g.astype(jnp.float32)[:, None, :], 0.0).reshape(shape)
    hi_out[...] = spread(hi).astype(jnp.bfloat16)
    lo_out[...] = spread(lo).astype(jnp.bfloat16)
    extended[:, :feature] = tokens[...]
    extended[:, feature:] = jnp.concatenate(
        [hi.astype(jnp.float32), lo.astype(jnp.float32)], axis=1
    ).astype(jnp.bfloat16)
    step = 128
    for c in range(0, send.shape[1], step):
        send[:, c : c + step] = dot_f32(one_hot, tokens[:, c : c + step]).astype(jnp.bfloat16)


def prepare_ring(members, e0, e1, e2, e3, send, hi_out, lo_out, rows_out):
    tok, width = e0.shape
    feature = rows_out.shape[1]
    blocks = 4
    n_experts = hi_out.shape[0] // (blocks * CAP)
    first = feature - send.shape[1]
    parts = []
    his = []
    los = []
    for j, e in enumerate((e0, e1, e2, e3)):
        rows_out[j * tok : (j + 1) * tok, :] = e[:, :feature]
        meta = e[:, feature:].astype(jnp.float32)
        hi = meta[:, :tok]
        his.append(hi)
        los.append(meta[:, tok:])
        parts.append(slot_codes(hi > 0))
    code = jnp.concatenate(parts, axis=1)
    hi = jnp.concatenate(his, axis=1)
    lo = jnp.concatenate(los, axis=1)
    rows = blocks * tok
    chunk = 16
    shape = (chunk, blocks * CAP, rows)
    slot = lax.broadcasted_iota(jnp.int32, shape, 1)
    at = lax.broadcasted_iota(jnp.int32, shape, 2)
    block = slot // CAP
    odd = lax.broadcasted_iota(jnp.int32, shape, 0) // members % 2 == 1
    block = jnp.where(odd & (block == 1), 2, jnp.where(odd & (block == 2), 1, block))
    want = jnp.where(at // tok == block, slot % CAP, -2).astype(jnp.float32)
    flat = chunk * blocks * CAP
    for c in range(0, n_experts, chunk):
        hit = code[c : c + chunk, None, :] == want
        out = slice(c * blocks * CAP, c * blocks * CAP + flat)
        one_hot = jnp.where(hit, 1.0, 0.0).reshape(flat, rows).astype(jnp.bfloat16)
        spread = lambda g: (
            jnp.where(hit, g[c : c + chunk, None, :], 0.0).reshape(flat, rows).astype(jnp.bfloat16)
        )
        hi_out[out, :] = spread(hi)
        lo_out[out, :] = spread(lo)
        send[out, :] = dot_f32(one_hot, rows_out[:, first:]).astype(jnp.bfloat16)


def call_prepare_own(count, ids, weights, tokens, n_experts, cols):
    tok, feature = tokens.shape
    slots = n_experts * CAP
    return pl.pallas_call(
        prepare_own,
        in_specs=[pl.BlockSpec(memory_space=pltpu.SMEM)] + [pl.BlockSpec()] * 3,
        out_shape=[
            jax.ShapeDtypeStruct((tok, feature + 2 * tok), jnp.bfloat16),
            hbm((slots, cols)),
            hbm((slots, tok)),
            hbm((slots, tok)),
        ],
        compiler_params=pltpu.CompilerParams(vmem_limit_bytes=24 * 1024 * 1024),
        name="prepare_own",
    )(count, *from_hbm(ids, weights, tokens))


def call_prepare_ring(around, members, n_experts, feature, cols):
    tok = around[0].shape[0]
    rows = len(around) * tok
    slots = n_experts * CAP * len(around)
    return pl.pallas_call(
        functools.partial(prepare_ring, members),
        out_shape=[
            hbm((slots, cols)),
            hbm((slots, rows)),
            hbm((slots, rows)),
            hbm((rows, feature)),
        ],
        compiler_params=pltpu.CompilerParams(vmem_limit_bytes=24 * 1024 * 1024),
        name="prepare_ring",
    )(*around)


def expert_kernel(planes, pair, *refs):
    n_x = planes * 2
    xin, (xb, wg, wu, wd) = refs[:n_x], refs[n_x : n_x + 4]
    members = wg.shape[0]
    n_out = members + 1
    rest = refs[len(refs) - (n_out + 10) :]
    outs, ob = rest[:n_out], rest[n_out]
    xbb, obb, obuf, wgb, wub, wdb, xs, in_sems, out_sems = rest[n_out + 1 :]
    rows, sc = xin[0].shape
    bc = outs[0].shape[-1]
    feature = wg.shape[2]
    n_ep = xb.shape[0]
    slots = planes * CAP
    pairs = xb.shape[1] // (members * slots)
    fetched, sent = [], []

    def fetch(src, dst):
        copy = pltpu.make_async_copy(src, dst, in_sems.at[len(fetched)])
        copy.start()
        fetched.append(copy)
        return copy

    def send(src, dst):
        copy = pltpu.make_async_copy(src, dst, out_sems.at[len(sent)])
        copy.start()
        sent.append(copy)

    chunk = lambda m: pl.ds((m * pairs + pair) * slots, slots)
    got = []
    for m in range(members):
        copies = [
            fetch(xin[p * members + m], xs.at[m, pl.ds(p * rows, rows), pl.ds(0, sc)])
            for p in range(planes)
        ]
        copies.append(fetch(xb.at[:, chunk(m)], xbb.at[m]))
        copies += [fetch(w.at[m], buf.at[m]) for w, buf in ((wg, wgb), (wu, wub), (wd, wdb))]
        got.append(copies)
    for m in range(members):
        for copy in got[m][: planes + 1]:
            copy.wait()
        for c in range(0, feature - sc, COLS):
            part = xbb[m, :, :, c : c + COLS].astype(jnp.float32).reshape(n_ep, planes, CAP, COLS)
            for p in range(planes):
                xs[m, p * rows : (p + 1) * rows, sc + c : sc + c + COLS] = (
                    part[:, p].reshape(rows, COLS).astype(jnp.bfloat16)
                )
        got[m][planes + 1].wait()
        gate = lax.dot_general(wgb[m], xs[m], NT, preferred_element_type=jnp.float32)
        got[m][planes + 2].wait()
        up = lax.dot_general(wub[m], xs[m], NT, preferred_element_type=jnp.float32)
        hidden = (gate / (1.0 + jnp.exp(-gate)) * up).astype(jnp.bfloat16)
        got[m][planes + 3].wait()
        out = lax.dot_general(hidden, wdb[m], TN, preferred_element_type=jnp.float32)
        for p in range(planes):
            obuf[m, p] = out[p * rows : (p + 1) * rows, :bc].astype(jnp.bfloat16)
            send(obuf.at[m, p], outs[m] if p == 0 else outs[-1].at[pl.ds(m * rows, rows)])
        for c in range(0, feature - bc, COLS):
            part = out[:, bc + c : bc + c + COLS].reshape(planes, n_ep, CAP, COLS)
            part = jnp.stack([part[p] for p in range(planes)], axis=1)
            obb[m, :, :, c : c + COLS] = part.reshape(n_ep, slots, COLS).astype(jnp.bfloat16)
        send(obb.at[m], ob.at[:, chunk(m)])
    for copy in sent:
        copy.wait()


def run_experts(planes, pair, xb, sofar, wg, wu, wd, back):
    members, ffe, feature = wg.shape
    xin = [x for plane in planes for x in plane]
    n_ep, slots, cols_b = xb.shape
    step = len(planes) * CAP
    rows = len(planes) * n_ep * CAP
    bf = jnp.bfloat16
    out_x = [hbm((n_ep * CAP, back))] * members + [hbm((members * n_ep * CAP, back))]
    operands = from_hbm(*xin, xb, wg, wu, wd)
    aliases = {}
    if sofar is not None:
        aliases = {len(operands): len(out_x)}
        operands.append(sofar)
    return pl.pallas_call(
        functools.partial(expert_kernel, len(planes), pair),
        in_specs=[pl.BlockSpec(memory_space=pltpu.HBM)] * len(operands),
        out_specs=[pl.BlockSpec(memory_space=pltpu.HBM)] * (len(out_x) + 1),
        out_shape=out_x + [hbm((n_ep, slots, feature - back))],
        scratch_shapes=[
            pltpu.VMEM((members, n_ep, step, cols_b), bf),
            pltpu.VMEM((members, n_ep, step, feature - back), bf),
            pltpu.VMEM((members, len(planes), n_ep * CAP, back), bf),
            pltpu.VMEM((members, ffe, feature), bf),
            pltpu.VMEM((members, ffe, feature), bf),
            pltpu.VMEM((members, ffe, feature), bf),
            pltpu.VMEM((members, rows, feature), bf),
            pltpu.SemaphoreType.DMA((members * (len(planes) + 4),)),
            pltpu.SemaphoreType.DMA((members * (len(planes) + 1),)),
        ],
        input_output_aliases=aliases,
        compiler_params=pltpu.CompilerParams(vmem_limit_bytes=VMEM_LIMIT),
        cost_estimate=pl.CostEstimate(
            flops=20 * 10**9, bytes_accessed=20 * 10**7, transcendentals=0
        ),
        name="experts",
    )(*operands)


def last_sum(own, *refs):
    ends, out = refs[:-1], refs[-1]
    n_ep, slots, cols = out.shape
    rows = n_ep * CAP
    for c in range(0, cols, COLS):
        parts = []
        for m, end in enumerate(ends):
            mine = own[m * rows : (m + 1) * rows, c : c + COLS].astype(jnp.float32)
            came = end[:, c : c + COLS].astype(jnp.float32)
            parts.append((mine + came).reshape(n_ep, CAP, COLS))
        out[:, :, c : c + COLS] = (
            jnp.stack(parts, axis=1).reshape(n_ep, slots, COLS).astype(jnp.bfloat16)
        )


def call_last_sum(own, ends, n_ep):
    rows, cols = own.shape
    slots = len(ends) * CAP
    block = lambda n: pl.BlockSpec((n, WIDE), lambda c: (0, c))
    return pl.pallas_call(
        last_sum,
        grid=(cols // WIDE,),
        in_specs=[block(rows)] + [block(x.shape[0]) for x in ends],
        out_specs=pl.BlockSpec((n_ep, slots, WIDE), lambda c: (0, 0, c)),
        out_shape=hbm((n_ep, slots, cols)),
        compiler_params=pltpu.CompilerParams(vmem_limit_bytes=16 * 1024 * 1024),
        name="last_sum",
    )(*from_hbm(own, *ends))


def weigh(hi, lo, values):
    return dot_f32(hi, values) + dot_f32(lo, values)


def combine(hi, lo, values, shared, *outs):
    tok = outs[0].shape[0]
    total = shared[...] + weigh(hi[...], lo[...], values[...])
    for j, o in enumerate(outs):
        o[...] = total[j * tok : (j + 1) * tok].astype(jnp.bfloat16)


def call_combine(hi, lo, values, shared, tok):
    rows, slots = hi.shape
    cols = values.shape[1]
    whole = pl.BlockSpec((rows, slots), lambda c: (0, 0))
    block = lambda n: pl.BlockSpec((n, WIDE), lambda c: (0, c))
    return pl.pallas_call(
        combine,
        grid=(cols // WIDE,),
        in_specs=[whole, whole, block(slots), block(rows)],
        out_specs=[block(tok)] * (rows // tok),
        out_shape=[jax.ShapeDtypeStruct((tok, cols), jnp.bfloat16)] * (rows // tok),
        compiler_params=pltpu.CompilerParams(vmem_limit_bytes=24 * 1024 * 1024),
        name="combine",
    )(*from_hbm(hi, lo, values), shared)


def finish(hi, lo, values, early, late, out):
    here = pl.program_id(0)
    routed_blocks = pl.num_programs(0) - pl.cdiv(late.shape[1], WIDE)

    @pl.when(here < routed_blocks)
    def _():
        out[...] = (early[...] + weigh(hi[...], lo[...], values[...])).astype(jnp.bfloat16)

    @pl.when(here >= routed_blocks)
    def _():
        at = pl.multiple_of((here - routed_blocks) * WIDE, WIDE)
        out[...] = late[:, pl.ds(at, WIDE)]


def call_finish(hi, lo, values, early, late):
    tok, slots = hi.shape
    bc = values.shape[1]
    cols = bc + late.shape[1]
    last = bc // WIDE - 1
    whole = lambda shape: pl.BlockSpec(shape, lambda c: (0, 0))
    block = lambda n: pl.BlockSpec((n, WIDE), lambda c: (0, jnp.minimum(c, last)))
    return pl.pallas_call(
        finish,
        grid=(cols // WIDE,),
        in_specs=[whole((tok, slots))] * 2 + [block(slots), block(tok), whole(late.shape)],
        out_specs=pl.BlockSpec((tok, WIDE), lambda c: (0, c)),
        out_shape=jax.ShapeDtypeStruct((tok, cols), jnp.bfloat16),
        compiler_params=pltpu.CompilerParams(vmem_limit_bytes=16 * 1024 * 1024),
        name="finish",
    )(hi, lo, *from_hbm(values), early, late)


def on_device(
    tokens,
    row_counts,
    expert_ids,
    gate_weights,
    expert_gate,
    expert_up,
    expert_down,
    shared_gate,
    shared_up,
    shared_down,
):
    tok, feature = tokens.shape
    members = expert_gate.shape[0]
    n_ep = lax.axis_size("ep")
    n_dp = lax.axis_size("dp")
    n_experts = members * n_ep
    sc, bc = SEND_COLS, BACK_COLS

    def over_ep(x, rows, cols):
        return lax.all_to_all(
            x.reshape(n_ep, rows, cols), "ep", split_axis=0, concat_axis=0, tiled=True
        )

    extended, send_d, hi_d, lo_d = call_prepare_own(
        row_counts, expert_ids.T, gate_weights.T, tokens, n_experts, sc
    )
    own = over_ep(send_d, members * CAP, sc)

    around = [shifted(extended, s) for s in AROUND] + [extended]
    send_b, hi_b, lo_b, gathered = call_prepare_ring(
        around, members, n_experts, feature, feature - sc
    )

    weights = (expert_gate.swapaxes(1, 2), expert_up.swapaxes(1, 2), expert_down)

    own_slots = own.reshape(n_ep, members, CAP, sc)
    own_parts = [own_slots[:, m].reshape(n_ep * CAP, sc) for m in range(members)]
    behind = [toward(x) for x in own_parts]

    gate_act = dot_f32(gathered, shared_gate)
    up_act = dot_f32(gathered, shared_up)
    hidden = (jax.nn.silu(gate_act) * up_act).astype(jnp.bfloat16)
    shared = dot_f32(hidden, shared_down)
    behind[0], shared = lax.optimization_barrier((behind[0], shared))
    far = [toward(x) for x in behind]
    ahead = [toward(x) for x in far]
    came_b = over_ep(send_b, members * n_dp * CAP, feature - sc)

    *to_far, to_behind, out_b = run_experts([far, behind], 0, came_b, None, *weights, bc)
    f32 = lambda x: x.astype(jnp.float32)
    early = shared[:, :bc].astype(jnp.bfloat16).reshape(n_dp, tok, bc)
    early = [shifted(early[j], -s) for j, s in enumerate(AROUND)] + [early[n_dp - 1]]
    *to_ahead, to_own, out_b = run_experts([ahead, own_parts], 1, came_b, out_b, *weights, bc)
    ret_b = over_ep(out_b, members * n_dp * CAP, feature - bc)

    rows = n_ep * CAP
    arrived = toward(to_behind)
    ends = []
    for m in range(members):
        part = slice(m * rows, (m + 1) * rows)
        passing = (f32(to_far[m]) + f32(arrived[part])).astype(jnp.bfloat16)
        passing = (f32(to_ahead[m]) + f32(toward(passing))).astype(jnp.bfloat16)
        ends.append(toward(passing))
    *ends, late, hi_b, lo_b, hi_d, lo_d = lax.optimization_barrier(
        (*ends, shared[:, bc:], hi_b.T, lo_b.T, hi_d.T, lo_d.T)
    )
    back_d = call_last_sum(to_own, ends, n_ep)
    back_d, ret_b = lax.optimization_barrier((back_d, ret_b))
    ret_d = over_ep(back_d, members * CAP, bc)

    live = jnp.arange(tok, dtype=jnp.int32) < row_counts[0]
    early = jnp.where(live[:, None], sum(f32(x) for x in early), 0.0)
    *parts, late = call_combine(hi_b, lo_b, ret_b.reshape(-1, feature - bc), late, tok)
    late = f32(late) + sum(f32(shifted(x, -s)) for x, s in zip(parts, AROUND))
    late = jnp.where(live[:, None], late, 0.0).astype(jnp.bfloat16)
    return call_finish(hi_d, lo_d, ret_d.reshape(-1, bc), early, late)


def solution(mesh):
    in_specs = (
        P(("dp", "ep"), None),
        P(("dp", "ep")),
        P(("dp", "ep"), None),
        P(("dp", "ep"), None),
        P("ep", None, "dp"),
        P("ep", None, "dp"),
        P("ep", "dp", None),
        P(None, "dp"),
        P(None, "dp"),
        P("dp", None),
    )
    out_specs = P(("dp", "ep"), None)
    return jax.shard_map(
        on_device, mesh=mesh, in_specs=in_specs, out_specs=out_specs, check_vma=False
    )
```

```python
import functools

import jax
import jax.numpy as jnp
from jax import lax
from jax.experimental import pallas as pl
from jax.experimental.pallas import tpu as pltpu
from jax.sharding import PartitionSpec as P

CAP = 8
SEND_COLS = 1280
BACK_COLS = 1280
COLS = 128
NT = (((1,), (1,)), ((), ()))
TN = (((0,), (0,)), ((), ()))
AROUND = (2, 1, -1)
VMEM_LIMIT = 40 * 1024 * 1024


def shifted(x, shift):
    n = lax.axis_size("dp")
    return lax.ppermute(x, "dp", [(i, (i + shift) % n) for i in range(n)])


def toward(x):
    n, m = lax.axis_size("dp"), lax.axis_size("ep")
    pairs = []
    for i in range(n):
        for e in range(m):
            step = 1 if e % 2 == 0 else -1
            pairs.append((i * m + e, (i + step) % n * m + e))
    return lax.ppermute(x, ("dp", "ep"), pairs)


def hbm(shape):
    return pltpu.HBM(shape, jnp.bfloat16)


def from_hbm(*arrays):
    return [pltpu.with_memory_space_constraint(x, pltpu.HBM) for x in arrays]


def dot_f32(a, b):
    return jnp.dot(a, b, preferred_element_type=jnp.float32)


def split_hi_lo(x):
    hi = x.astype(jnp.bfloat16)
    lo = (x - hi.astype(jnp.float32)).astype(jnp.bfloat16)
    return hi, lo


def slot_codes(used):
    tok = used.shape[1]
    before = lax.broadcasted_iota(jnp.int32, (tok, tok), 0) < lax.broadcasted_iota(
        jnp.int32, (tok, tok), 1
    )
    ones = jnp.where(used, 1.0, 0.0)
    rank = dot_f32(
        ones.astype(jnp.bfloat16), jnp.where(before, 1.0, 0.0).astype(jnp.bfloat16)
    )
    return jnp.where(used, rank, -1.0)


def prepare_own(count, ids, weights, tokens, extended, send, hi_out, lo_out):
    top, tok = ids.shape
    feature = tokens.shape[1]
    n_experts = hi_out.shape[0] // CAP
    expert = lax.broadcasted_iota(jnp.int32, (n_experts, tok), 0)
    gates = jnp.zeros((n_experts, tok), jnp.float32)
    for k in range(top):
        gates = gates + jnp.where(expert == ids[k : k + 1, :], weights[k : k + 1, :], 0.0)
    live = lax.broadcasted_iota(jnp.int32, (n_experts, tok), 1) < count[0]
    gates = jnp.where(live, gates, 0.0)
    hi, lo = split_hi_lo(gates)
    code = slot_codes(gates > 0)
    want = lax.broadcasted_iota(jnp.int32, (n_experts, CAP, tok), 1).astype(jnp.float32)
    hit = code[:, None, :] == want
    shape = (n_experts * CAP, tok)
    one_hot = jnp.where(hit, 1.0, 0.0).reshape(shape).astype(jnp.bfloat16)
    spread = lambda g: jnp.where(hit, g.astype(jnp.float32)[:, None, :], 0.0).reshape(shape)
    hi_out[...] = spread(hi).astype(jnp.bfloat16)
    lo_out[...] = spread(lo).astype(jnp.bfloat16)
    extended[:, :feature] = tokens[...]
    extended[:, feature:] = jnp.concatenate(
        [hi.astype(jnp.float32), lo.astype(jnp.float32)], axis=1
    ).astype(jnp.bfloat16)
    step = 128
    for c in range(0, send.shape[1], step):
        send[:, c : c + step] = dot_f32(one_hot, tokens[:, c : c + step]).astype(jnp.bfloat16)


def prepare_ring(members, e0, e1, e2, e3, send, hi_out, lo_out, rows_out):
    tok, width = e0.shape
    feature = rows_out.shape[1]
    blocks = 4
    n_experts = hi_out.shape[0] // (blocks * CAP)
    first = feature - send.shape[1]
    parts = []
    his = []
    los = []
    for j, e in enumerate((e0, e1, e2, e3)):
        rows_out[j * tok : (j + 1) * tok, :] = e[:, :feature]
        meta = e[:, feature:].astype(jnp.float32)
        hi = meta[:, :tok]
        his.append(hi)
        los.append(meta[:, tok:])
        parts.append(slot_codes(hi > 0))
    code = jnp.concatenate(parts, axis=1)
    hi = jnp.concatenate(his, axis=1)
    lo = jnp.concatenate(los, axis=1)
    rows = blocks * tok
    chunk = 16
    shape = (chunk, blocks * CAP, rows)
    slot = lax.broadcasted_iota(jnp.int32, shape, 1)
    at = lax.broadcasted_iota(jnp.int32, shape, 2)
    block = slot // CAP
    odd = lax.broadcasted_iota(jnp.int32, shape, 0) // members % 2 == 1
    block = jnp.where(odd & (block == 1), 2, jnp.where(odd & (block == 2), 1, block))
    want = jnp.where(at // tok == block, slot % CAP, -2).astype(jnp.float32)
    flat = chunk * blocks * CAP
    for c in range(0, n_experts, chunk):
        hit = code[c : c + chunk, None, :] == want
        out = slice(c * blocks * CAP, c * blocks * CAP + flat)
        one_hot = jnp.where(hit, 1.0, 0.0).reshape(flat, rows).astype(jnp.bfloat16)
        spread = lambda g: (
            jnp.where(hit, g[c : c + chunk, None, :], 0.0).reshape(flat, rows).astype(jnp.bfloat16)
        )
        hi_out[out, :] = spread(hi)
        lo_out[out, :] = spread(lo)
        send[out, :] = dot_f32(one_hot, rows_out[:, first:]).astype(jnp.bfloat16)


def call_prepare_own(count, ids, weights, tokens, n_experts, cols):
    tok, feature = tokens.shape
    slots = n_experts * CAP
    return pl.pallas_call(
        prepare_own,
        in_specs=[pl.BlockSpec(memory_space=pltpu.SMEM)] + [pl.BlockSpec()] * 3,
        out_shape=[
            jax.ShapeDtypeStruct((tok, feature + 2 * tok), jnp.bfloat16),
            hbm((slots, cols)),
            hbm((slots, tok)),
            hbm((slots, tok)),
        ],
        compiler_params=pltpu.CompilerParams(vmem_limit_bytes=24 * 1024 * 1024),
        name="prepare_own",
    )(count, *from_hbm(ids, weights, tokens))


def call_prepare_ring(around, members, n_experts, feature, cols):
    tok = around[0].shape[0]
    rows = len(around) * tok
    slots = n_experts * CAP * len(around)
    return pl.pallas_call(
        functools.partial(prepare_ring, members),
        out_shape=[
            hbm((slots, cols)),
            hbm((slots, rows)),
            hbm((slots, rows)),
            hbm((rows, feature)),
        ],
        compiler_params=pltpu.CompilerParams(vmem_limit_bytes=24 * 1024 * 1024),
        name="prepare_ring",
    )(*around)


def expert_kernel(planes, pair, *refs):
    n_x = planes * 2
    xin, (xb, wg, wu, wd) = refs[:n_x], refs[n_x : n_x + 4]
    members = wg.shape[0]
    n_out = members + 1
    rest = refs[len(refs) - (n_out + 10) :]
    outs, ob = rest[:n_out], rest[n_out]
    xbb, obb, obuf, wgb, wub, wdb, xs, in_sems, out_sems = rest[n_out + 1 :]
    rows, sc = xin[0].shape
    bc = outs[0].shape[-1]
    feature = wg.shape[2]
    n_ep = xb.shape[0]
    slots = planes * CAP
    pairs = xb.shape[1] // (members * slots)
    fetched, sent = [], []

    def fetch(src, dst):
        copy = pltpu.make_async_copy(src, dst, in_sems.at[len(fetched)])
        copy.start()
        fetched.append(copy)
        return copy

    def send(src, dst):
        copy = pltpu.make_async_copy(src, dst, out_sems.at[len(sent)])
        copy.start()
        sent.append(copy)

    chunk = lambda m: pl.ds((m * pairs + pair) * slots, slots)
    got = []
    for m in range(members):
        copies = [
            fetch(xin[p * members + m], xs.at[m, pl.ds(p * rows, rows), pl.ds(0, sc)])
            for p in range(planes)
        ]
        copies.append(fetch(xb.at[:, chunk(m)], xbb.at[m]))
        copies += [fetch(w.at[m], buf.at[m]) for w, buf in ((wg, wgb), (wu, wub), (wd, wdb))]
        got.append(copies)
    for m in range(members):
        for copy in got[m][: planes + 1]:
            copy.wait()
        for c in range(0, feature - sc, COLS):
            part = xbb[m, :, :, c : c + COLS].astype(jnp.float32).reshape(n_ep, planes, CAP, COLS)
            for p in range(planes):
                xs[m, p * rows : (p + 1) * rows, sc + c : sc + c + COLS] = (
                    part[:, p].reshape(rows, COLS).astype(jnp.bfloat16)
                )
        got[m][planes + 1].wait()
        gate = lax.dot_general(wgb[m], xs[m], NT, preferred_element_type=jnp.float32)
        got[m][planes + 2].wait()
        up = lax.dot_general(wub[m], xs[m], NT, preferred_element_type=jnp.float32)
        hidden = (gate / (1.0 + jnp.exp(-gate)) * up).astype(jnp.bfloat16)
        got[m][planes + 3].wait()
        out = lax.dot_general(hidden, wdb[m], TN, preferred_element_type=jnp.float32)
        for p in range(planes):
            obuf[m, p] = out[p * rows : (p + 1) * rows, :bc].astype(jnp.bfloat16)
            send(obuf.at[m, p], outs[m] if p == 0 else outs[-1].at[pl.ds(m * rows, rows)])
        for c in range(0, feature - bc, COLS):
            part = out[:, bc + c : bc + c + COLS].reshape(planes, n_ep, CAP, COLS)
            part = jnp.stack([part[p] for p in range(planes)], axis=1)
            obb[m, :, :, c : c + COLS] = part.reshape(n_ep, slots, COLS).astype(jnp.bfloat16)
        send(obb.at[m], ob.at[:, chunk(m)])
    for copy in sent:
        copy.wait()


def run_experts(planes, pair, xb, sofar, wg, wu, wd, back):
    members, ffe, feature = wg.shape
    xin = [x for plane in planes for x in plane]
    n_ep, slots, cols_b = xb.shape
    step = len(planes) * CAP
    rows = len(planes) * n_ep * CAP
    bf = jnp.bfloat16
    out_x = [hbm((n_ep * CAP, back))] * members + [hbm((members * n_ep * CAP, back))]
    operands = from_hbm(*xin, xb, wg, wu, wd)
    aliases = {}
    if sofar is not None:
        aliases = {len(operands): len(out_x)}
        operands.append(sofar)
    return pl.pallas_call(
        functools.partial(expert_kernel, len(planes), pair),
        in_specs=[pl.BlockSpec(memory_space=pltpu.HBM)] * len(operands),
        out_specs=[pl.BlockSpec(memory_space=pltpu.HBM)] * (len(out_x) + 1),
        out_shape=out_x + [hbm((n_ep, slots, feature - back))],
        scratch_shapes=[
            pltpu.VMEM((members, n_ep, step, cols_b), bf),
            pltpu.VMEM((members, n_ep, step, feature - back), bf),
            pltpu.VMEM((members, len(planes), n_ep * CAP, back), bf),
            pltpu.VMEM((members, ffe, feature), bf),
            pltpu.VMEM((members, ffe, feature), bf),
            pltpu.VMEM((members, ffe, feature), bf),
            pltpu.VMEM((members, rows, feature), bf),
            pltpu.SemaphoreType.DMA((members * (len(planes) + 4),)),
            pltpu.SemaphoreType.DMA((members * (len(planes) + 1),)),
        ],
        input_output_aliases=aliases,
        compiler_params=pltpu.CompilerParams(vmem_limit_bytes=VMEM_LIMIT),
        cost_estimate=pl.CostEstimate(
            flops=20 * 10**9, bytes_accessed=20 * 10**7, transcendentals=0
        ),
        name="experts",
    )(*operands)


def last_sum(own, *refs):
    ends, out = refs[:-1], refs[-1]
    sources, slots, cols = out.shape
    for c in range(0, cols, COLS):
        parts = []
        for m, end in enumerate(ends):
            mine = own[m, :, c : c + COLS].astype(jnp.float32)
            came = end[:, c : c + COLS].astype(jnp.float32)
            parts.append((mine + came).reshape(sources, CAP, COLS))
        out[:, :, c : c + COLS] = (
            jnp.stack(parts, axis=1).reshape(sources, slots, COLS).astype(jnp.bfloat16)
        )


def call_last_sum(own, ends, n_ep):
    members, cols = len(ends), own.shape[1]
    steps = 4
    rows = n_ep * CAP // steps
    return pl.pallas_call(
        last_sum,
        grid=(steps,),
        in_specs=[pl.BlockSpec((members, rows, cols), lambda i: (0, i, 0))]
        + [pl.BlockSpec((rows, cols), lambda i: (i, 0))] * members,
        out_specs=pl.BlockSpec((n_ep // steps, members * CAP, cols), lambda i: (i, 0, 0)),
        out_shape=hbm((n_ep, members * CAP, cols)),
        compiler_params=pltpu.CompilerParams(vmem_limit_bytes=16 * 1024 * 1024),
        name="last_sum",
    )(*from_hbm(own.reshape(members, n_ep * CAP, cols), *ends))


def weigh(hi, lo, values):
    return dot_f32(hi, values) + dot_f32(lo, values)


def combine(hi, lo, values, shared, *refs):
    outs, total = refs[:-1], refs[-1]
    tok = outs[0].shape[0]
    here = pl.program_id(0)
    part = weigh(hi[...], lo[...], values[...])

    @pl.when(here == 0)
    def _():
        total[...] = shared[...] + part

    @pl.when(here > 0)
    def _():
        total[...] = total[...] + part

    @pl.when(here == pl.num_programs(0) - 1)
    def _():
        for j, o in enumerate(outs):
            o[...] = total[j * tok : (j + 1) * tok].astype(jnp.bfloat16)


def call_combine(hi, lo, values, shared, tok):
    rows, slots = hi.shape
    cols = values.shape[1]
    steps = 4
    left = pl.BlockSpec((rows, slots // steps), lambda i: (0, i))
    return pl.pallas_call(
        combine,
        grid=(steps,),
        in_specs=[
            left,
            left,
            pl.BlockSpec((slots // steps, cols), lambda i: (i, 0)),
            pl.BlockSpec((rows, cols), lambda i: (0, 0)),
        ],
        out_specs=[pl.BlockSpec((tok, cols), lambda i: (0, 0))] * (rows // tok),
        out_shape=[jax.ShapeDtypeStruct((tok, cols), jnp.bfloat16)] * (rows // tok),
        scratch_shapes=[pltpu.VMEM((rows, cols), jnp.float32)],
        compiler_params=pltpu.CompilerParams(vmem_limit_bytes=24 * 1024 * 1024),
        name="combine",
    )(*from_hbm(hi, lo, values, shared))


def finish(hi, lo, values, early, late, out):
    bc = values.shape[1]
    out[:, bc:] = late[...]
    out[:, :bc] = (early[...] + weigh(hi[...], lo[...], values[...])).astype(jnp.bfloat16)


def call_finish(hi, lo, values, early, late):
    return pl.pallas_call(
        finish,
        out_shape=jax.ShapeDtypeStruct(
            (hi.shape[0], values.shape[1] + late.shape[1]), jnp.bfloat16
        ),
        compiler_params=pltpu.CompilerParams(vmem_limit_bytes=16 * 1024 * 1024),
        name="finish",
    )(hi, lo, *from_hbm(values), early, late)


def on_device(
    tokens,
    row_counts,
    expert_ids,
    gate_weights,
    expert_gate,
    expert_up,
    expert_down,
    shared_gate,
    shared_up,
    shared_down,
):
    tok, feature = tokens.shape
    members = expert_gate.shape[0]
    n_ep = lax.axis_size("ep")
    n_dp = lax.axis_size("dp")
    n_experts = members * n_ep
    sc, bc = SEND_COLS, BACK_COLS

    def over_ep(x, rows, cols):
        return lax.all_to_all(
            x.reshape(n_ep, rows, cols), "ep", split_axis=0, concat_axis=0, tiled=True
        )

    extended, send_d, hi_d, lo_d = call_prepare_own(
        row_counts, expert_ids.T, gate_weights.T, tokens, n_experts, sc
    )
    own = over_ep(send_d, members * CAP, sc)

    around = [shifted(extended, s) for s in AROUND] + [extended]
    send_b, hi_b, lo_b, gathered = call_prepare_ring(
        around, members, n_experts, feature, feature - sc
    )

    weights = (expert_gate.swapaxes(1, 2), expert_up.swapaxes(1, 2), expert_down)

    own_slots = own.reshape(n_ep, members, CAP, sc)
    own_parts = [own_slots[:, m].reshape(n_ep * CAP, sc) for m in range(members)]
    behind = [toward(x) for x in own_parts]

    gate_act = dot_f32(gathered, shared_gate)
    up_act = dot_f32(gathered, shared_up)
    hidden = (jax.nn.silu(gate_act) * up_act).astype(jnp.bfloat16)
    shared = dot_f32(hidden, shared_down)
    behind[0], shared = lax.optimization_barrier((behind[0], shared))
    far = [toward(x) for x in behind]
    ahead = [toward(x) for x in far]
    came_b = over_ep(send_b, members * n_dp * CAP, feature - sc)

    *to_far, to_behind, out_b = run_experts([far, behind], 0, came_b, None, *weights, bc)
    f32 = lambda x: x.astype(jnp.float32)
    early = shared[:, :bc].astype(jnp.bfloat16).reshape(n_dp, tok, bc)
    early = [early[j] for j in range(n_dp)]
    *to_ahead, to_own, out_b = run_experts([ahead, own_parts], 1, came_b, out_b, *weights, bc)
    ret_b = over_ep(out_b, members * n_dp * CAP, feature - bc)

    rows = n_ep * CAP
    arrived = toward(to_behind)
    ends = []
    for m in range(members):
        part = slice(m * rows, (m + 1) * rows)
        passing = (f32(to_far[m]) + f32(arrived[part])).astype(jnp.bfloat16)
        passing = (f32(to_ahead[m]) + f32(toward(passing))).astype(jnp.bfloat16)
        ends.append(toward(passing))
    ends, early, late, hi_b, lo_b, hi_d, lo_d = lax.optimization_barrier(
        (ends, early, shared[:, bc:], hi_b.T, lo_b.T, hi_d.T, lo_d.T)
    )
    back_d = call_last_sum(to_own, ends, n_ep)
    back_d, ret_b = lax.optimization_barrier((back_d, ret_b))
    ret_d = over_ep(back_d, members * CAP, bc)

    live = jnp.arange(tok, dtype=jnp.int32) < row_counts[0]
    early = [shifted(x, -s) for x, s in zip(early, AROUND)] + [early[-1]]
    early = jnp.where(live[:, None], sum(f32(x) for x in early), 0.0)
    *parts, late = call_combine(hi_b, lo_b, ret_b.reshape(-1, feature - bc), late, tok)
    late = f32(late) + sum(f32(shifted(x, -s)) for x, s in zip(parts, AROUND))
    late = jnp.where(live[:, None], late, 0.0).astype(jnp.bfloat16)
    return call_finish(hi_d, lo_d, ret_d.reshape(-1, bc), early, late)


def solution(mesh):
    in_specs = (
        P(("dp", "ep"), None),
        P(("dp", "ep")),
        P(("dp", "ep"), None),
        P(("dp", "ep"), None),
        P("ep", None, "dp"),
        P("ep", None, "dp"),
        P("ep", "dp", None),
        P(None, "dp"),
        P(None, "dp"),
        P("dp", None),
    )
    out_specs = P(("dp", "ep"), None)
    return jax.shard_map(
        on_device, mesh=mesh, in_specs=in_specs, out_specs=out_specs, check_vma=False
    )
```

```python
import functools

import jax
import jax.numpy as jnp
from jax import lax
from jax.experimental import pallas as pl
from jax.experimental.pallas import tpu as pltpu
from jax.sharding import PartitionSpec as P

CAP = 8
SEND_COLS = 1280
BACK_COLS = 1280
COLS = 128
NT = (((1,), (1,)), ((), ()))
TN = (((0,), (0,)), ((), ()))
AROUND = (2, 1, -1)
VMEM_LIMIT = 40 * 1024 * 1024


def shifted(x, shift):
    n = lax.axis_size("dp")
    return lax.ppermute(x, "dp", [(i, (i + shift) % n) for i in range(n)])


def toward(x):
    n, m = lax.axis_size("dp"), lax.axis_size("ep")
    pairs = []
    for i in range(n):
        for e in range(m):
            step = 1 if e % 2 == 0 else -1
            pairs.append((i * m + e, (i + step) % n * m + e))
    return lax.ppermute(x, ("dp", "ep"), pairs)


def hbm(shape):
    return pltpu.HBM(shape, jnp.bfloat16)


def from_hbm(*arrays):
    return [pltpu.with_memory_space_constraint(x, pltpu.HBM) for x in arrays]


def dot_f32(a, b):
    return jnp.dot(a, b, preferred_element_type=jnp.float32)


def split_hi_lo(x):
    hi = x.astype(jnp.bfloat16)
    lo = (x - hi.astype(jnp.float32)).astype(jnp.bfloat16)
    return hi, lo


def slot_codes(used):
    tok = used.shape[1]
    before = lax.broadcasted_iota(jnp.int32, (tok, tok), 0) < lax.broadcasted_iota(
        jnp.int32, (tok, tok), 1
    )
    ones = jnp.where(used, 1.0, 0.0)
    rank = dot_f32(
        ones.astype(jnp.bfloat16), jnp.where(before, 1.0, 0.0).astype(jnp.bfloat16)
    )
    return jnp.where(used, rank, -1.0)


def prepare_own(count, ids, weights, tokens, extended, send, hi_out, lo_out):
    top, tok = ids.shape
    feature = tokens.shape[1]
    n_experts = hi_out.shape[0] // CAP
    expert = lax.broadcasted_iota(jnp.int32, (n_experts, tok), 0)
    gates = jnp.zeros((n_experts, tok), jnp.float32)
    for k in range(top):
        gates = gates + jnp.where(expert == ids[k : k + 1, :], weights[k : k + 1, :], 0.0)
    live = lax.broadcasted_iota(jnp.int32, (n_experts, tok), 1) < count[0]
    gates = jnp.where(live, gates, 0.0)
    hi, lo = split_hi_lo(gates)
    code = slot_codes(gates > 0)
    want = lax.broadcasted_iota(jnp.int32, (n_experts, CAP, tok), 1).astype(jnp.float32)
    hit = code[:, None, :] == want
    shape = (n_experts * CAP, tok)
    one_hot = jnp.where(hit, 1.0, 0.0).reshape(shape).astype(jnp.bfloat16)
    spread = lambda g: jnp.where(hit, g.astype(jnp.float32)[:, None, :], 0.0).reshape(shape)
    hi_out[...] = spread(hi).astype(jnp.bfloat16)
    lo_out[...] = spread(lo).astype(jnp.bfloat16)
    extended[:, :feature] = tokens[...]
    extended[:, feature:] = jnp.concatenate(
        [hi.astype(jnp.float32), lo.astype(jnp.float32)], axis=1
    ).astype(jnp.bfloat16)
    step = 128
    for c in range(0, send.shape[1], step):
        send[:, c : c + step] = dot_f32(one_hot, tokens[:, c : c + step]).astype(jnp.bfloat16)


def prepare_ring(members, e0, e1, e2, e3, send, hi_out, lo_out, rows_out):
    tok, width = e0.shape
    feature = rows_out.shape[1]
    blocks = 4
    n_experts = hi_out.shape[0] // (blocks * CAP)
    first = feature - send.shape[1]
    parts = []
    his = []
    los = []
    for j, e in enumerate((e0, e1, e2, e3)):
        rows_out[j * tok : (j + 1) * tok, :] = e[:, :feature]
        meta = e[:, feature:].astype(jnp.float32)
        hi = meta[:, :tok]
        his.append(hi)
        los.append(meta[:, tok:])
        parts.append(slot_codes(hi > 0))
    code = jnp.concatenate(parts, axis=1)
    hi = jnp.concatenate(his, axis=1)
    lo = jnp.concatenate(los, axis=1)
    rows = blocks * tok
    chunk = 16
    shape = (chunk, blocks * CAP, rows)
    slot = lax.broadcasted_iota(jnp.int32, shape, 1)
    at = lax.broadcasted_iota(jnp.int32, shape, 2)
    block = slot // CAP
    odd = lax.broadcasted_iota(jnp.int32, shape, 0) // members % 2 == 1
    block = jnp.where(odd & (block == 1), 2, jnp.where(odd & (block == 2), 1, block))
    want = jnp.where(at // tok == block, slot % CAP, -2).astype(jnp.float32)
    flat = chunk * blocks * CAP
    for c in range(0, n_experts, chunk):
        hit = code[c : c + chunk, None, :] == want
        out = slice(c * blocks * CAP, c * blocks * CAP + flat)
        one_hot = jnp.where(hit, 1.0, 0.0).reshape(flat, rows).astype(jnp.bfloat16)
        spread = lambda g: (
            jnp.where(hit, g[c : c + chunk, None, :], 0.0).reshape(flat, rows).astype(jnp.bfloat16)
        )
        hi_out[out, :] = spread(hi)
        lo_out[out, :] = spread(lo)
        send[out, :] = dot_f32(one_hot, rows_out[:, first:]).astype(jnp.bfloat16)


def call_prepare_own(count, ids, weights, tokens, n_experts, cols):
    tok, feature = tokens.shape
    slots = n_experts * CAP
    return pl.pallas_call(
        prepare_own,
        in_specs=[pl.BlockSpec(memory_space=pltpu.SMEM)] + [pl.BlockSpec()] * 3,
        out_shape=[
            jax.ShapeDtypeStruct((tok, feature + 2 * tok), jnp.bfloat16),
            hbm((slots, cols)),
            hbm((slots, tok)),
            hbm((slots, tok)),
        ],
        compiler_params=pltpu.CompilerParams(vmem_limit_bytes=24 * 1024 * 1024),
        name="prepare_own",
    )(count, *from_hbm(ids, weights, tokens))


def call_prepare_ring(around, members, n_experts, feature, cols):
    tok = around[0].shape[0]
    rows = len(around) * tok
    slots = n_experts * CAP * len(around)
    return pl.pallas_call(
        functools.partial(prepare_ring, members),
        out_shape=[
            hbm((slots, cols)),
            hbm((slots, rows)),
            hbm((slots, rows)),
            hbm((rows, feature)),
        ],
        compiler_params=pltpu.CompilerParams(vmem_limit_bytes=24 * 1024 * 1024),
        name="prepare_ring",
    )(*around)


def expert_kernel(planes, pair, *refs):
    n_x = planes * 2
    xin, (xb, wg, wu, wd) = refs[:n_x], refs[n_x : n_x + 4]
    members = wg.shape[0]
    n_out = members + 1
    rest = refs[len(refs) - (n_out + 10) :]
    outs, ob = rest[:n_out], rest[n_out]
    xbb, obb, obuf, wgb, wub, wdb, xs, in_sems, out_sems = rest[n_out + 1 :]
    rows, sc = xin[0].shape
    bc = outs[0].shape[-1]
    feature = wg.shape[2]
    n_ep = xb.shape[0]
    slots = planes * CAP
    pairs = xb.shape[1] // (members * slots)
    fetched, sent = [], []

    def fetch(src, dst):
        copy = pltpu.make_async_copy(src, dst, in_sems.at[len(fetched)])
        copy.start()
        fetched.append(copy)
        return copy

    def send(src, dst):
        copy = pltpu.make_async_copy(src, dst, out_sems.at[len(sent)])
        copy.start()
        sent.append(copy)

    chunk = lambda m: pl.ds((m * pairs + pair) * slots, slots)
    got = []
    for m in range(members):
        copies = [
            fetch(xin[p * members + m], xs.at[m, pl.ds(p * rows, rows), pl.ds(0, sc)])
            for p in range(planes)
        ]
        copies.append(fetch(xb.at[:, chunk(m)], xbb.at[m]))
        copies += [fetch(w.at[m], buf.at[m]) for w, buf in ((wg, wgb), (wu, wub), (wd, wdb))]
        got.append(copies)
    for m in range(members):
        for copy in got[m][: planes + 1]:
            copy.wait()
        for c in range(0, feature - sc, COLS):
            part = xbb[m, :, :, c : c + COLS].astype(jnp.float32).reshape(n_ep, planes, CAP, COLS)
            for p in range(planes):
                xs[m, p * rows : (p + 1) * rows, sc + c : sc + c + COLS] = (
                    part[:, p].reshape(rows, COLS).astype(jnp.bfloat16)
                )
        got[m][planes + 1].wait()
        gate = lax.dot_general(wgb[m], xs[m], NT, preferred_element_type=jnp.float32)
        got[m][planes + 2].wait()
        up = lax.dot_general(wub[m], xs[m], NT, preferred_element_type=jnp.float32)
        hidden = (gate / (1.0 + jnp.exp(-gate)) * up).astype(jnp.bfloat16)
        got[m][planes + 3].wait()
        out = lax.dot_general(hidden, wdb[m], TN, preferred_element_type=jnp.float32)
        for p in range(planes):
            obuf[m, p] = out[p * rows : (p + 1) * rows, :bc].astype(jnp.bfloat16)
            send(obuf.at[m, p], outs[m] if p == 0 else outs[-1].at[pl.ds(m * rows, rows)])
        for c in range(0, feature - bc, COLS):
            part = out[:, bc + c : bc + c + COLS].reshape(planes, n_ep, CAP, COLS)
            part = jnp.stack([part[p] for p in range(planes)], axis=1)
            obb[m, :, :, c : c + COLS] = part.reshape(n_ep, slots, COLS).astype(jnp.bfloat16)
        send(obb.at[m], ob.at[:, chunk(m)])
    for copy in sent:
        copy.wait()


def run_experts(planes, pair, xb, sofar, wg, wu, wd, back):
    members, ffe, feature = wg.shape
    xin = [x for plane in planes for x in plane]
    n_ep, slots, cols_b = xb.shape
    step = len(planes) * CAP
    rows = len(planes) * n_ep * CAP
    bf = jnp.bfloat16
    out_x = [hbm((n_ep * CAP, back))] * members + [hbm((members * n_ep * CAP, back))]
    operands = from_hbm(*xin, xb, wg, wu, wd)
    aliases = {}
    if sofar is not None:
        aliases = {len(operands): len(out_x)}
        operands.append(sofar)
    return pl.pallas_call(
        functools.partial(expert_kernel, len(planes), pair),
        in_specs=[pl.BlockSpec(memory_space=pltpu.HBM)] * len(operands),
        out_specs=[pl.BlockSpec(memory_space=pltpu.HBM)] * (len(out_x) + 1),
        out_shape=out_x + [hbm((n_ep, slots, feature - back))],
        scratch_shapes=[
            pltpu.VMEM((members, n_ep, step, cols_b), bf),
            pltpu.VMEM((members, n_ep, step, feature - back), bf),
            pltpu.VMEM((members, len(planes), n_ep * CAP, back), bf),
            pltpu.VMEM((members, ffe, feature), bf),
            pltpu.VMEM((members, ffe, feature), bf),
            pltpu.VMEM((members, ffe, feature), bf),
            pltpu.VMEM((members, rows, feature), bf),
            pltpu.SemaphoreType.DMA((members * (len(planes) + 4),)),
            pltpu.SemaphoreType.DMA((members * (len(planes) + 1),)),
        ],
        input_output_aliases=aliases,
        compiler_params=pltpu.CompilerParams(vmem_limit_bytes=VMEM_LIMIT),
        cost_estimate=pl.CostEstimate(
            flops=20 * 10**9, bytes_accessed=20 * 10**7, transcendentals=0
        ),
        name="experts",
    )(*operands)


def last_sum(own, *refs):
    ends, out = refs[:-1], refs[-1]
    n_ep, slots, cols = out.shape
    rows = n_ep * CAP
    for c in range(0, cols, COLS):
        parts = []
        for m, end in enumerate(ends):
            mine = own[m * rows : (m + 1) * rows, c : c + COLS].astype(jnp.float32)
            came = end[:, c : c + COLS].astype(jnp.float32)
            parts.append((mine + came).reshape(n_ep, CAP, COLS))
        out[:, :, c : c + COLS] = (
            jnp.stack(parts, axis=1).reshape(n_ep, slots, COLS).astype(jnp.bfloat16)
        )


def call_last_sum(own, ends, n_ep):
    return pl.pallas_call(
        last_sum,
        out_shape=hbm((n_ep, len(ends) * CAP, own.shape[1])),
        compiler_params=pltpu.CompilerParams(vmem_limit_bytes=16 * 1024 * 1024),
        name="last_sum",
    )(*from_hbm(own, *ends))


def weigh(hi, lo, values):
    return dot_f32(hi, values) + dot_f32(lo, values)


def combine(hi, lo, values, shared, *refs):
    outs, total = refs[:-1], refs[-1]
    tok = outs[0].shape[0]
    here = pl.program_id(0)
    part = weigh(hi[...], lo[...], values[...])

    @pl.when(here == 0)
    def _():
        total[...] = shared[...] + part

    @pl.when(here > 0)
    def _():
        total[...] = total[...] + part

    @pl.when(here == pl.num_programs(0) - 1)
    def _():
        for j, o in enumerate(outs):
            o[...] = total[j * tok : (j + 1) * tok].astype(jnp.bfloat16)


def call_combine(hi, lo, values, shared, tok):
    rows, slots = hi.shape
    cols = values.shape[1]
    steps = 4
    left = pl.BlockSpec((rows, slots // steps), lambda i: (0, i))
    return pl.pallas_call(
        combine,
        grid=(steps,),
        in_specs=[
            left,
            left,
            pl.BlockSpec((slots // steps, cols), lambda i: (i, 0)),
            pl.BlockSpec((rows, cols), lambda i: (0, 0)),
        ],
        out_specs=[pl.BlockSpec((tok, cols), lambda i: (0, 0))] * (rows // tok),
        out_shape=[jax.ShapeDtypeStruct((tok, cols), jnp.bfloat16)] * (rows // tok),
        scratch_shapes=[pltpu.VMEM((rows, cols), jnp.float32)],
        compiler_params=pltpu.CompilerParams(vmem_limit_bytes=24 * 1024 * 1024),
        name="combine",
    )(*from_hbm(hi, lo, values, shared))


def finish(hi, lo, values, early, late, out):
    bc = values.shape[1]
    out[:, bc:] = late[...]
    out[:, :bc] = (early[...] + weigh(hi[...], lo[...], values[...])).astype(jnp.bfloat16)


def call_finish(hi, lo, values, early, late):
    return pl.pallas_call(
        finish,
        out_shape=jax.ShapeDtypeStruct(
            (hi.shape[0], values.shape[1] + late.shape[1]), jnp.bfloat16
        ),
        compiler_params=pltpu.CompilerParams(vmem_limit_bytes=16 * 1024 * 1024),
        name="finish",
    )(hi, lo, *from_hbm(values), early, late)


def on_device(
    tokens,
    row_counts,
    expert_ids,
    gate_weights,
    expert_gate,
    expert_up,
    expert_down,
    shared_gate,
    shared_up,
    shared_down,
):
    tok, feature = tokens.shape
    members = expert_gate.shape[0]
    n_ep = lax.axis_size("ep")
    n_dp = lax.axis_size("dp")
    n_experts = members * n_ep
    sc, bc = SEND_COLS, BACK_COLS

    def over_ep(x, rows, cols):
        return lax.all_to_all(
            x.reshape(n_ep, rows, cols), "ep", split_axis=0, concat_axis=0, tiled=True
        )

    extended, send_d, hi_d, lo_d = call_prepare_own(
        row_counts, expert_ids.T, gate_weights.T, tokens, n_experts, sc
    )
    own = over_ep(send_d, members * CAP, sc)

    around = [shifted(extended, s) for s in AROUND] + [extended]
    send_b, hi_b, lo_b, gathered = call_prepare_ring(
        around, members, n_experts, feature, feature - sc
    )

    weights = (expert_gate.swapaxes(1, 2), expert_up.swapaxes(1, 2), expert_down)

    own_parts = []
    for m in range(members):
        own_slots = own.reshape(n_ep, members, CAP, sc)
        own_parts.append(own_slots[:, m].reshape(n_ep * CAP, sc))
        own, own_parts[m] = lax.optimization_barrier((own, own_parts[m]))
    behind = [toward(x) for x in own_parts]

    gate_act = dot_f32(gathered, shared_gate)
    up_act = dot_f32(gathered, shared_up)
    hidden = (jax.nn.silu(gate_act) * up_act).astype(jnp.bfloat16)
    shared = dot_f32(hidden, shared_down)
    behind[0], shared = lax.optimization_barrier((behind[0], shared))
    far = [toward(x) for x in behind]
    ahead = [toward(x) for x in far]
    came_b = over_ep(send_b, members * n_dp * CAP, feature - sc)

    *to_far, to_behind, out_b = run_experts([far, behind], 0, came_b, None, *weights, bc)
    f32 = lambda x: x.astype(jnp.float32)
    early = shared[:, :bc].astype(jnp.bfloat16).reshape(n_dp, tok, bc)
    early = [early[j] for j in range(n_dp)]
    *to_ahead, to_own, out_b = run_experts([ahead, own_parts], 1, came_b, out_b, *weights, bc)
    ret_b = over_ep(out_b, members * n_dp * CAP, feature - bc)

    rows = n_ep * CAP
    arrived = toward(to_behind)
    ends = []
    for m in range(members):
        part = slice(m * rows, (m + 1) * rows)
        passing = (f32(to_far[m]) + f32(arrived[part])).astype(jnp.bfloat16)
        passing = (f32(to_ahead[m]) + f32(toward(passing))).astype(jnp.bfloat16)
        ends.append(toward(passing))
    ends, early, late, hi_b, lo_b, hi_d, lo_d = lax.optimization_barrier(
        (ends, early, shared[:, bc:], hi_b.T, lo_b.T, hi_d.T, lo_d.T)
    )
    back_d = call_last_sum(to_own, ends, n_ep)
    back_d, ret_b = lax.optimization_barrier((back_d, ret_b))
    ret_d = over_ep(back_d, members * CAP, bc)

    live = jnp.arange(tok, dtype=jnp.int32) < row_counts[0]
    early = [shifted(x, -s) for x, s in zip(early, AROUND)] + [early[-1]]
    early = jnp.where(live[:, None], sum(f32(x) for x in early), 0.0)
    *parts, late = call_combine(hi_b, lo_b, ret_b.reshape(-1, feature - bc), late, tok)
    late = f32(late) + sum(f32(shifted(x, -s)) for x, s in zip(parts, AROUND))
    late = jnp.where(live[:, None], late, 0.0).astype(jnp.bfloat16)
    return call_finish(hi_d, lo_d, ret_d.reshape(-1, bc), early, late)


def solution(mesh):
    in_specs = (
        P(("dp", "ep"), None),
        P(("dp", "ep")),
        P(("dp", "ep"), None),
        P(("dp", "ep"), None),
        P("ep", None, "dp"),
        P("ep", None, "dp"),
        P("ep", "dp", None),
        P(None, "dp"),
        P(None, "dp"),
        P("dp", None),
    )
    out_specs = P(("dp", "ep"), None)
    return jax.shard_map(
        on_device, mesh=mesh, in_specs=in_specs, out_specs=out_specs, check_vma=False
    )
```

```python
import functools

import jax
import jax.numpy as jnp
from jax import lax
from jax.experimental import pallas as pl
from jax.experimental.pallas import tpu as pltpu
from jax.sharding import PartitionSpec as P

CAP = 8
SEND_COLS = 1280
BACK_COLS = 1280
COLS = 128
NT = (((1,), (1,)), ((), ()))
TN = (((0,), (0,)), ((), ()))
AROUND = (2, 1, -1)
VMEM_LIMIT = 40 * 1024 * 1024


def shifted(x, shift):
    n = lax.axis_size("dp")
    return lax.ppermute(x, "dp", [(i, (i + shift) % n) for i in range(n)])


def toward(x):
    n, m = lax.axis_size("dp"), lax.axis_size("ep")
    pairs = []
    for i in range(n):
        for e in range(m):
            step = 1 if e % 2 == 0 else -1
            pairs.append((i * m + e, (i + step) % n * m + e))
    return lax.ppermute(x, ("dp", "ep"), pairs)


def hbm(shape):
    return pltpu.HBM(shape, jnp.bfloat16)


def from_hbm(*arrays):
    return [pltpu.with_memory_space_constraint(x, pltpu.HBM) for x in arrays]


def dot_f32(a, b):
    return jnp.dot(a, b, preferred_element_type=jnp.float32)


def split_hi_lo(x):
    hi = x.astype(jnp.bfloat16)
    lo = (x - hi.astype(jnp.float32)).astype(jnp.bfloat16)
    return hi, lo


def slot_codes(used):
    tok = used.shape[1]
    before = lax.broadcasted_iota(jnp.int32, (tok, tok), 0) < lax.broadcasted_iota(
        jnp.int32, (tok, tok), 1
    )
    ones = jnp.where(used, 1.0, 0.0)
    rank = dot_f32(
        ones.astype(jnp.bfloat16), jnp.where(before, 1.0, 0.0).astype(jnp.bfloat16)
    )
    return jnp.where(used, rank, -1.0)


def prepare_own(count, ids, weights, tokens, extended, send, hi_out, lo_out):
    top, tok = ids.shape
    feature = tokens.shape[1]
    n_experts = hi_out.shape[0] // CAP
    expert = lax.broadcasted_iota(jnp.int32, (n_experts, tok), 0)
    gates = jnp.zeros((n_experts, tok), jnp.float32)
    for k in range(top):
        gates = gates + jnp.where(expert == ids[k : k + 1, :], weights[k : k + 1, :], 0.0)
    live = lax.broadcasted_iota(jnp.int32, (n_experts, tok), 1) < count[0]
    gates = jnp.where(live, gates, 0.0)
    hi, lo = split_hi_lo(gates)
    code = slot_codes(gates > 0)
    want = lax.broadcasted_iota(jnp.int32, (n_experts, CAP, tok), 1).astype(jnp.float32)
    hit = code[:, None, :] == want
    shape = (n_experts * CAP, tok)
    one_hot = jnp.where(hit, 1.0, 0.0).reshape(shape).astype(jnp.bfloat16)
    spread = lambda g: jnp.where(hit, g.astype(jnp.float32)[:, None, :], 0.0).reshape(shape)
    hi_out[...] = spread(hi).astype(jnp.bfloat16)
    lo_out[...] = spread(lo).astype(jnp.bfloat16)
    extended[:, :feature] = tokens[...]
    extended[:, feature:] = jnp.concatenate(
        [hi.astype(jnp.float32), lo.astype(jnp.float32)], axis=1
    ).astype(jnp.bfloat16)
    step = 128
    for c in range(0, send.shape[1], step):
        send[:, c : c + step] = dot_f32(one_hot, tokens[:, c : c + step]).astype(jnp.bfloat16)


def prepare_ring(members, e0, e1, e2, e3, send, hi_out, lo_out, rows_out):
    tok, width = e0.shape
    feature = rows_out.shape[1]
    blocks = 4
    n_experts = hi_out.shape[0] // (blocks * CAP)
    first = feature - send.shape[1]
    parts = []
    his = []
    los = []
    for j, e in enumerate((e0, e1, e2, e3)):
        rows_out[j * tok : (j + 1) * tok, :] = e[:, :feature]
        meta = e[:, feature:].astype(jnp.float32)
        hi = meta[:, :tok]
        his.append(hi)
        los.append(meta[:, tok:])
        parts.append(slot_codes(hi > 0))
    code = jnp.concatenate(parts, axis=1)
    hi = jnp.concatenate(his, axis=1)
    lo = jnp.concatenate(los, axis=1)
    rows = blocks * tok
    chunk = 16
    shape = (chunk, blocks * CAP, rows)
    slot = lax.broadcasted_iota(jnp.int32, shape, 1)
    at = lax.broadcasted_iota(jnp.int32, shape, 2)
    block = slot // CAP
    odd = lax.broadcasted_iota(jnp.int32, shape, 0) // members % 2 == 1
    block = jnp.where(odd & (block == 1), 2, jnp.where(odd & (block == 2), 1, block))
    want = jnp.where(at // tok == block, slot % CAP, -2).astype(jnp.float32)
    flat = chunk * blocks * CAP
    for c in range(0, n_experts, chunk):
        hit = code[c : c + chunk, None, :] == want
        out = slice(c * blocks * CAP, c * blocks * CAP + flat)
        one_hot = jnp.where(hit, 1.0, 0.0).reshape(flat, rows).astype(jnp.bfloat16)
        spread = lambda g: (
            jnp.where(hit, g[c : c + chunk, None, :], 0.0).reshape(flat, rows).astype(jnp.bfloat16)
        )
        hi_out[out, :] = spread(hi)
        lo_out[out, :] = spread(lo)
        send[out, :] = dot_f32(one_hot, rows_out[:, first:]).astype(jnp.bfloat16)


def call_prepare_own(count, ids, weights, tokens, n_experts, cols):
    tok, feature = tokens.shape
    slots = n_experts * CAP
    return pl.pallas_call(
        prepare_own,
        in_specs=[pl.BlockSpec(memory_space=pltpu.SMEM)] + [pl.BlockSpec()] * 3,
        out_shape=[
            jax.ShapeDtypeStruct((tok, feature + 2 * tok), jnp.bfloat16),
            hbm((slots, cols)),
            hbm((slots, tok)),
            hbm((slots, tok)),
        ],
        compiler_params=pltpu.CompilerParams(vmem_limit_bytes=24 * 1024 * 1024),
        name="prepare_own",
    )(count, *from_hbm(ids, weights, tokens))


def call_prepare_ring(around, members, n_experts, feature, cols):
    tok = around[0].shape[0]
    rows = len(around) * tok
    slots = n_experts * CAP * len(around)
    return pl.pallas_call(
        functools.partial(prepare_ring, members),
        out_shape=[
            hbm((slots, cols)),
            hbm((slots, rows)),
            hbm((slots, rows)),
            hbm((rows, feature)),
        ],
        compiler_params=pltpu.CompilerParams(vmem_limit_bytes=24 * 1024 * 1024),
        name="prepare_ring",
    )(*around)


def expert_kernel(planes, pair, *refs):
    n_x = planes * 2
    xin, (xb, wg, wu, wd) = refs[:n_x], refs[n_x : n_x + 4]
    members = wg.shape[0]
    n_out = members + 1
    rest = refs[len(refs) - (n_out + 10) :]
    outs, ob = rest[:n_out], rest[n_out]
    xbb, obb, obuf, wgb, wub, wdb, xs, in_sems, out_sems = rest[n_out + 1 :]
    rows, sc = xin[0].shape
    bc = outs[0].shape[-1]
    feature = wg.shape[2]
    n_ep = xb.shape[0]
    slots = planes * CAP
    pairs = xb.shape[1] // (members * slots)
    fetched, sent = [], []

    def fetch(src, dst):
        copy = pltpu.make_async_copy(src, dst, in_sems.at[len(fetched)])
        copy.start()
        fetched.append(copy)
        return copy

    def send(src, dst):
        copy = pltpu.make_async_copy(src, dst, out_sems.at[len(sent)])
        copy.start()
        sent.append(copy)

    chunk = lambda m: pl.ds((m * pairs + pair) * slots, slots)
    got = []
    for m in range(members):
        copies = [
            fetch(xin[p * members + m], xs.at[m, pl.ds(p * rows, rows), pl.ds(0, sc)])
            for p in range(planes)
        ]
        copies.append(fetch(xb.at[:, chunk(m)], xbb.at[m]))
        copies += [fetch(w.at[m], buf.at[m]) for w, buf in ((wg, wgb), (wu, wub), (wd, wdb))]
        got.append(copies)
    for m in range(members):
        for copy in got[m][: planes + 1]:
            copy.wait()
        for c in range(0, feature - sc, COLS):
            part = xbb[m, :, :, c : c + COLS].astype(jnp.float32).reshape(n_ep, planes, CAP, COLS)
            for p in range(planes):
                xs[m, p * rows : (p + 1) * rows, sc + c : sc + c + COLS] = (
                    part[:, p].reshape(rows, COLS).astype(jnp.bfloat16)
                )
        got[m][planes + 1].wait()
        gate = lax.dot_general(wgb[m], xs[m], NT, preferred_element_type=jnp.float32)
        got[m][planes + 2].wait()
        up = lax.dot_general(wub[m], xs[m], NT, preferred_element_type=jnp.float32)
        hidden = (gate / (1.0 + jnp.exp(-gate)) * up).astype(jnp.bfloat16)
        got[m][planes + 3].wait()
        out = lax.dot_general(hidden, wdb[m], TN, preferred_element_type=jnp.float32)
        for p in range(planes):
            obuf[m, p] = out[p * rows : (p + 1) * rows, :bc].astype(jnp.bfloat16)
            send(obuf.at[m, p], outs[m] if p == 0 else outs[-1].at[pl.ds(m * rows, rows)])
        for c in range(0, feature - bc, COLS):
            part = out[:, bc + c : bc + c + COLS].reshape(planes, n_ep, CAP, COLS)
            part = jnp.stack([part[p] for p in range(planes)], axis=1)
            obb[m, :, :, c : c + COLS] = part.reshape(n_ep, slots, COLS).astype(jnp.bfloat16)
        send(obb.at[m], ob.at[:, chunk(m)])
    for copy in sent:
        copy.wait()


def run_experts(planes, pair, xb, sofar, wg, wu, wd, back):
    members, ffe, feature = wg.shape
    xin = [x for plane in planes for x in plane]
    n_ep, slots, cols_b = xb.shape
    step = len(planes) * CAP
    rows = len(planes) * n_ep * CAP
    bf = jnp.bfloat16
    out_x = [hbm((n_ep * CAP, back))] * members + [hbm((members * n_ep * CAP, back))]
    operands = from_hbm(*xin, xb, wg, wu, wd)
    aliases = {}
    if sofar is not None:
        aliases = {len(operands): len(out_x)}
        operands.append(sofar)
    return pl.pallas_call(
        functools.partial(expert_kernel, len(planes), pair),
        in_specs=[pl.BlockSpec(memory_space=pltpu.HBM)] * len(operands),
        out_specs=[pl.BlockSpec(memory_space=pltpu.HBM)] * (len(out_x) + 1),
        out_shape=out_x + [hbm((n_ep, slots, feature - back))],
        scratch_shapes=[
            pltpu.VMEM((members, n_ep, step, cols_b), bf),
            pltpu.VMEM((members, n_ep, step, feature - back), bf),
            pltpu.VMEM((members, len(planes), n_ep * CAP, back), bf),
            pltpu.VMEM((members, ffe, feature), bf),
            pltpu.VMEM((members, ffe, feature), bf),
            pltpu.VMEM((members, ffe, feature), bf),
            pltpu.VMEM((members, rows, feature), bf),
            pltpu.SemaphoreType.DMA((members * (len(planes) + 4),)),
            pltpu.SemaphoreType.DMA((members * (len(planes) + 1),)),
        ],
        input_output_aliases=aliases,
        compiler_params=pltpu.CompilerParams(vmem_limit_bytes=VMEM_LIMIT),
        cost_estimate=pl.CostEstimate(
            flops=20 * 10**9, bytes_accessed=20 * 10**7, transcendentals=0
        ),
        name="experts",
    )(*operands)


def last_sum(own, *refs):
    ends, out = refs[:-1], refs[-1]
    n_ep, slots, cols = out.shape
    rows = n_ep * CAP
    for c in range(0, cols, COLS):
        parts = []
        for m, end in enumerate(ends):
            mine = own[m * rows : (m + 1) * rows, c : c + COLS].astype(jnp.float32)
            came = end[:, c : c + COLS].astype(jnp.float32)
            parts.append((mine + came).reshape(n_ep, CAP, COLS))
        out[:, :, c : c + COLS] = (
            jnp.stack(parts, axis=1).reshape(n_ep, slots, COLS).astype(jnp.bfloat16)
        )


def call_last_sum(own, ends, n_ep):
    return pl.pallas_call(
        last_sum,
        out_shape=hbm((n_ep, len(ends) * CAP, own.shape[1])),
        compiler_params=pltpu.CompilerParams(vmem_limit_bytes=16 * 1024 * 1024),
        name="last_sum",
    )(*from_hbm(own, *ends))


def weigh(hi, lo, values):
    rows = hi.shape[0]
    both = dot_f32(jnp.concatenate([hi, lo], axis=0), values)
    return both[:rows] + both[rows:]


def combine(hi, lo, values, shared, *refs):
    outs, total = refs[:-1], refs[-1]
    tok = outs[0].shape[0]
    here = pl.program_id(0)
    part = weigh(hi[...], lo[...], values[...])

    @pl.when(here == 0)
    def _():
        total[...] = shared[...] + part

    @pl.when(here > 0)
    def _():
        total[...] = total[...] + part

    @pl.when(here == pl.num_programs(0) - 1)
    def _():
        for j, o in enumerate(outs):
            o[...] = total[j * tok : (j + 1) * tok].astype(jnp.bfloat16)


def call_combine(hi, lo, values, shared, tok):
    rows, slots = hi.shape
    cols = values.shape[1]
    steps = 4
    left = pl.BlockSpec((rows, slots // steps), lambda i: (0, i))
    return pl.pallas_call(
        combine,
        grid=(steps,),
        in_specs=[
            left,
            left,
            pl.BlockSpec((slots // steps, cols), lambda i: (i, 0)),
            pl.BlockSpec((rows, cols), lambda i: (0, 0)),
        ],
        out_specs=[pl.BlockSpec((tok, cols), lambda i: (0, 0))] * (rows // tok),
        out_shape=[jax.ShapeDtypeStruct((tok, cols), jnp.bfloat16)] * (rows // tok),
        scratch_shapes=[pltpu.VMEM((rows, cols), jnp.float32)],
        compiler_params=pltpu.CompilerParams(vmem_limit_bytes=24 * 1024 * 1024),
        name="combine",
    )(*from_hbm(hi, lo, values, shared))


def finish(hi, lo, values, early, late, out):
    bc = values.shape[1]
    out[:, bc:] = late[...]
    out[:, :bc] = (early[...] + weigh(hi[...], lo[...], values[...])).astype(jnp.bfloat16)


def call_finish(hi, lo, values, early, late):
    return pl.pallas_call(
        finish,
        out_shape=jax.ShapeDtypeStruct(
            (hi.shape[0], values.shape[1] + late.shape[1]), jnp.bfloat16
        ),
        compiler_params=pltpu.CompilerParams(vmem_limit_bytes=16 * 1024 * 1024),
        name="finish",
    )(hi, lo, *from_hbm(values), early, late)


def on_device(
    tokens,
    row_counts,
    expert_ids,
    gate_weights,
    expert_gate,
    expert_up,
    expert_down,
    shared_gate,
    shared_up,
    shared_down,
):
    tok, feature = tokens.shape
    members = expert_gate.shape[0]
    n_ep = lax.axis_size("ep")
    n_dp = lax.axis_size("dp")
    n_experts = members * n_ep
    sc, bc = SEND_COLS, BACK_COLS

    def over_ep(x, rows, cols):
        return lax.all_to_all(
            x.reshape(n_ep, rows, cols), "ep", split_axis=0, concat_axis=0, tiled=True
        )

    extended, send_d, hi_d, lo_d = call_prepare_own(
        row_counts, expert_ids.T, gate_weights.T, tokens, n_experts, sc
    )
    own = over_ep(send_d, members * CAP, sc)

    around = [shifted(extended, s) for s in AROUND] + [extended]
    send_b, hi_b, lo_b, gathered = call_prepare_ring(
        around, members, n_experts, feature, feature - sc
    )

    weights = (expert_gate.swapaxes(1, 2), expert_up.swapaxes(1, 2), expert_down)

    own_parts = []
    for m in range(members):
        own_slots = own.reshape(n_ep, members, CAP, sc)
        own_parts.append(own_slots[:, m].reshape(n_ep * CAP, sc))
        own, own_parts[m] = lax.optimization_barrier((own, own_parts[m]))
    behind = [toward(x) for x in own_parts]

    gate_act = dot_f32(gathered, shared_gate)
    up_act = dot_f32(gathered, shared_up)
    hidden = (jax.nn.silu(gate_act) * up_act).astype(jnp.bfloat16)
    shared = dot_f32(hidden, shared_down)
    behind[0], shared = lax.optimization_barrier((behind[0], shared))
    far = [toward(x) for x in behind]
    ahead = [toward(x) for x in far]
    came_b = over_ep(send_b, members * n_dp * CAP, feature - sc)

    *to_far, to_behind, out_b = run_experts([far, behind], 0, came_b, None, *weights, bc)
    f32 = lambda x: x.astype(jnp.float32)
    early = shared[:, :bc].astype(jnp.bfloat16).reshape(n_dp, tok, bc)
    early = [early[j] for j in range(n_dp)]
    *to_ahead, to_own, out_b = run_experts([ahead, own_parts], 1, came_b, out_b, *weights, bc)
    ret_b = over_ep(out_b, members * n_dp * CAP, feature - bc)

    rows = n_ep * CAP
    arrived = toward(to_behind)
    ends = []
    for m in range(members):
        part = slice(m * rows, (m + 1) * rows)
        passing = (f32(to_far[m]) + f32(arrived[part])).astype(jnp.bfloat16)
        passing = (f32(to_ahead[m]) + f32(toward(passing))).astype(jnp.bfloat16)
        ends.append(toward(passing))
    ends, early, late, hi_b, lo_b, hi_d, lo_d = lax.optimization_barrier(
        (ends, early, shared[:, bc:], hi_b.T, lo_b.T, hi_d.T, lo_d.T)
    )
    back_d = call_last_sum(to_own, ends, n_ep)
    back_d, ret_b = lax.optimization_barrier((back_d, ret_b))
    ret_d = over_ep(back_d, members * CAP, bc)

    live = jnp.arange(tok, dtype=jnp.int32) < row_counts[0]
    early = [shifted(x, -s) for x, s in zip(early, AROUND)] + [early[-1]]
    early = jnp.where(live[:, None], sum(f32(x) for x in early), 0.0)
    *parts, late = call_combine(hi_b, lo_b, ret_b.reshape(-1, feature - bc), late, tok)
    late = f32(late) + sum(f32(shifted(x, -s)) for x, s in zip(parts, AROUND))
    late = jnp.where(live[:, None], late, 0.0).astype(jnp.bfloat16)
    return call_finish(hi_d, lo_d, ret_d.reshape(-1, bc), early, late)


def solution(mesh):
    in_specs = (
        P(("dp", "ep"), None),
        P(("dp", "ep")),
        P(("dp", "ep"), None),
        P(("dp", "ep"), None),
        P("ep", None, "dp"),
        P("ep", None, "dp"),
        P("ep", "dp", None),
        P(None, "dp"),
        P(None, "dp"),
        P("dp", None),
    )
    out_specs = P(("dp", "ep"), None)
    return jax.shard_map(
        on_device, mesh=mesh, in_specs=in_specs, out_specs=out_specs, check_vma=False
    )
```
